512 devices in a mesh: row: 64 (over y, z), col: 8 (over x, core).
Axes of the slice: x: 4, y: 8, z: 8, core: 2. Of those that a mesh axis runs over, the one named last changes fastest.
Arguments:
- tokens: bfloat16 [2048, 6144], P(('row', 'col')), may hold values from -6 to 6
- norm_gain: float32 [6144], replicated, may hold values from 0.1 to 1.9
- in_weight: bfloat16 [6144, 24576], P('row', 'col'), may hold values from -0.078125 to 0.078125
- out_weight: bfloat16 [24576, 6144], P('row', 'col'), may hold values from -0.0390625 to 0.0390625
Outputs:
- block_out: bfloat16 [2048, 6144], P(('row', 'col'))
The draws below stay inside these ranges and needn't reach their ends.
All inputs are finite; a program needn't handle non-finite values.
Results may differ from the reference program's by a relative error of at most 0.0042.
Values may be sent and summed in bfloat16 or wider, within the bound.
A program may use at most 64 MiB of HBM per device.

```python
import jax
import jax.numpy as jnp
from jax import lax

D = 6144
FF = 24576
TOKENS = 2048


def shard_levels(own_key, dims, cuts, least, largest):
    gain, own = 1.0, jax.random.fold_in(own_key, 6)
    for axis_at, parts in cuts:
        heights = jnp.exp(jax.random.uniform(jax.random.fold_in(own, axis_at), (parts,), jnp.float32, least / len(cuts), largest / len(cuts)))
        gain = gain * jnp.repeat(heights, dims[axis_at] // parts).reshape([-1 if axis == axis_at else 1 for axis in range(len(dims))])
    return gain


def gaussian(own_key, extent, width, most, split=(), dtype=jnp.bfloat16):
    gain = shard_levels(own_key, extent, split, -0.22, 0.18) if split else 1.0
    drawn = jax.random.normal(own_key, extent, jnp.float32) * width * gain
    return jnp.minimum(jnp.maximum(drawn, -most), most).astype(dtype)


def setup_inputs(seed: int = 0) -> dict:
    key_of = jax.random.split(jax.random.key(seed), 5)
    return {
        "tokens": gaussian(key_of[0], (TOKENS, D), 1.0, 6.0, ((0, 512),)),
        "norm_gain": jnp.clip(1.0 + 0.18 * jax.random.normal(key_of[1], (D,), jnp.float32), 0.1, 1.9),
        "in_weight": gaussian(key_of[2], (D, FF), D ** -0.5, 0.078125, ((0, 64), (1, 8))),
        "out_weight": gaussian(key_of[3], (FF, D), FF ** -0.5, 0.0390625, ((0, 64), (1, 8))),
    }


def normalize(rows, norm_gain):
    values = rows.astype(jnp.float32)
    center = lax.optimization_barrier(jnp.mean(values, axis=1, keepdims=True))
    spread = lax.optimization_barrier(jnp.mean(jnp.square(values - center), axis=1, keepdims=True))
    scaled = (values - center) / jnp.sqrt(spread + 1e-06) * norm_gain.astype(jnp.float32)
    return scaled.astype(jnp.bfloat16)

def reference(tokens, norm_gain, in_weight, out_weight):
    normed = normalize(tokens, norm_gain)
    pre = jnp.dot(normed, in_weight, preferred_element_type=jnp.float32)
    hidden = jax.nn.gelu(pre, approximate=True).astype(jnp.bfloat16)
    branch = jnp.dot(hidden, out_weight, preferred_element_type=jnp.float32)
    return (tokens.astype(jnp.float32) + branch).astype(jnp.bfloat16)
```

```python
import jax
import jax.numpy as jnp
from jax import lax
from jax.experimental import pallas as pl
from jax.experimental.pallas import tpu as pltpu
from jax.sharding import PartitionSpec as P

MESH = pl.DeviceIdType.MESH
N = 8
BF16 = jnp.bfloat16
F32 = jnp.float32


def gelu(v):
    return 0.5 * v * (1.0 + jnp.tanh(0.7978845608028654 * (v + 0.044715 * (v * v * v))))


def rows_of(block):
    return block.reshape(block.shape[0] * block.shape[1], block.shape[2])


def kernel(
    tok_ref, gain_ref, inw_ref, outw_ref, out_ref,
    w1, w2, norm_out, norm_in, slab, x_buf, hid_out, h_buf,
    ring_send, ring_recv, part, part_in, own_part, fin_out, fin_in,
    w_sem, y_send, y_recv, w_send, w_recv, z_send, z_recv,
    xg_near, xg_relay, xg_sib, xg_recv, hg_near, hg_relay, hg_sib, hg_recv,
    ha_send, ha_recv, rs_send, rs_recv, p_send, p_recv, f_send, f_recv,
):
    row, c = lax.axis_index("row"), lax.axis_index("col")
    y, z = row // N, row % N
    x, core = c // 2, c % 2

    def dev(y_at, z_at, c_at):
        return (y_at * N + z_at, c_at)

    def col_of(x_at, core_at):
        return ((x_at + 8) % 4) * 2 + core_at

    def remote(src, dst, send, recv, target):
        return pltpu.make_async_remote_copy(
            src_ref=src, dst_ref=dst, send_sem=send, recv_sem=recv, device_id=target, device_id_type=MESH
        )

    right, left, across, sibling = col_of(x + 1, core), col_of(x - 1, core), col_of(x + 2, core), col_of(x, 1 - core)

    barrier = pltpu.get_barrier_semaphore()

    def greet(target):
        pl.semaphore_signal(barrier, inc=1, device_id=target, device_id_type=MESH)

    def greet_line(k, _):
        greet(dev((y + k) % N, z, c))
        greet(dev(y, (z + k) % N, c))
        return 0

    lax.fori_loop(1, N, greet_line, 0)
    for target in (right, left, sibling):
        greet(dev(y, z, target))

    def greet_plane(p, _):
        @pl.when(jnp.logical_or(y != c, p != c))
        def _():
            greet(dev(c, z, p))
            greet(dev(p, z, y))

        return 0

    lax.fori_loop(0, N, greet_plane, 0)

    own_w1 = pltpu.make_async_copy(inw_ref.at[:, pl.ds(pl.multiple_of(z * 384, 384), 384)], w1.at[z], w_sem.at[0])
    own_w1.start()
    own_w2 = [
        pltpu.make_async_copy(outw_ref.at[:, pl.ds(384 * j, 384)], w2.at[j], w_sem.at[1 + j]) for j in range(2)
    ]
    for copy in own_w2:
        copy.start()

    values = tok_ref[...].astype(F32)
    center = jnp.mean(values, axis=1, keepdims=True)
    spread = jnp.mean(jnp.square(values - center), axis=1, keepdims=True)
    normed = ((values - center) / jnp.sqrt(spread + 1e-06) * gain_ref[...]).astype(BF16)
    for j in range(N):
        norm_out[j] = normed[:, 768 * j : 768 * (j + 1)]
    norm_in[pl.ds(y, 1)] = norm_out[pl.ds(y, 1)]

    @pl.when(y == c)
    def _():
        pl.semaphore_wait(barrier, 31)

    @pl.when(y != c)
    def _():
        pl.semaphore_wait(barrier, 33)

    def y_copy(k):
        to = (y + k) % N
        return remote(norm_out.at[to], norm_in.at[y], y_send.at[k], y_recv.at[k], dev(to, z, c))

    def w_copy(k):
        to = (z + k) % N
        return remote(
            inw_ref.at[:, pl.ds(pl.multiple_of(to * 384, 384), 384)], w1.at[z], w_send.at[k], w_recv.at[k], dev(y, to, c)
        )

    def z_copy(k):
        to = (z + k) % N
        return remote(x_buf.at[c, z], x_buf.at[c, z], z_send.at[k], z_recv.at[k], dev(y, to, c))

    def over(start, make, act):
        def step(k, _):
            act(make(k))
            return 0

        lax.fori_loop(start, N, step, 0)

    over(1, y_copy, lambda copy: copy.start())
    over(1, w_copy, lambda copy: copy.start())
    over(1, y_copy, lambda copy: copy.wait_recv())
    for j in range(N):
        slab[4 * j : 4 * j + 4, 0:768] = norm_in[j].astype(F32)
    x_buf[c, z] = slab[:, 0:768].astype(BF16)
    over(1, z_copy, lambda copy: copy.start())

    def gather_cols(buf, ready, near, relay, sib, recv):
        def block(of, h):
            return buf.at[of, pl.ds(4 * h, 4)]

        def send(of, h, sem, target):
            copy = remote(block(of, h), block(of, h), sem, recv.at[of, h], dev(y, z, target))
            copy.start()
            return copy

        def arrived(of, h):
            remote(block(of, h), block(of, h), sib.at[0, 0], recv.at[of, h], dev(y, z, sibling)).wait_recv()

        sent = []
        for h in range(2):
            ready(h)
            sent.append(send(c, h, near.at[0, h], right))
            sent.append(send(c, h, near.at[1, h], left))
            sent.append(send(c, h, sib.at[0, h], sibling))
        arrived(left, 0)
        sent.append(send(left, 0, relay.at[0], right))
        arrived(right, 0)
        arrived(right, 1)
        sent.append(send(right, 1, relay.at[1], left))
        sent.append(send(left, 0, sib.at[1, 0], sibling))
        sent.append(send(right, 1, sib.at[2, 1], sibling))
        sent.append(send(right, 0, sib.at[2, 0], sibling))
        arrived(left, 1)
        sent.append(send(left, 1, sib.at[1, 1], sibling))
        for h in range(2):
            arrived(across, h)
            sent.append(send(across, h, sib.at[3, h], sibling))

        def rest():
            for d in range(4):
                for h in range(2):
                    arrived(col_of(x + d, 1 - core), h)

        return sent, rest

    def z_ready(h):
        def step(j, _):
            k = (z - j + N) % N

            @pl.when(k > 0)
            def _():
                z_copy(k).wait_recv()

            return 0

        lax.fori_loop(4 * h, 4 * h + 4, step, 0)

    sent_x, rest = gather_cols(x_buf, z_ready, xg_near, xg_relay, xg_sib, xg_recv)
    rest()
    own_w1.wait()
    over(1, w_copy, lambda copy: copy.wait_recv())

    def chain(q):
        h, back = q % 2, q // 2
        steps = 4 - (h + back) % 2
        return h, 1 - 2 * back, steps

    def ring_copy(at, q, s, place, neighbour):
        _, way, _ = chain(q)
        return remote(
            ring_send.at[at, q, s], ring_recv.at[at, q, s], rs_send.at[at, q, s], rs_recv.at[at, q, s],
            neighbour((place + way + N) % N),
        )

    def ring_step(at, q, s, place, neighbour, own):
        h, way, steps = chain(q)

        @pl.when(s < steps)
        def _():
            to = (place + way * (steps - s) + N) % N
            mine = own(to, h)

            @pl.when(s == 0)
            def _():
                ring_send[at, q, s] = mine.astype(BF16)

            @pl.when(s > 0)
            def _():
                before = jnp.maximum(s - 1, 0)
                ring_copy(at, q, before, place, neighbour).wait_recv()
                ring_send[at, q, s] = (mine + ring_recv[at, q, before].astype(F32)).astype(BF16)

            ring_copy(at, q, s, place, neighbour).start()

    def ring_last(at, h, place, neighbour, own):
        total = own(place, h)
        for q in (h, 2 + h):
            last = 3 - (h + q // 2) % 2
            ring_copy(at, q, last, place, neighbour).wait_recv()
            total = total + ring_recv[at, q, last].astype(F32)
        return total

    def rings(each):
        def step(i, _):
            for at, place, neighbour, own in each:
                ring_step(at, i % 4, i // 4, place, neighbour, own)
            return 0

        lax.fori_loop(0, 16, step, 0)

    def rings_sent(each):
        def step(i, _):
            for at, place, neighbour, own in each:
                q, s = i % 4, i // 4

                @pl.when(s < chain(q)[2])
                def _():
                    ring_copy(at, q, s, place, neighbour).wait_send()

            return 0

        lax.fori_loop(0, 16, step, 0)

    def along_y(to):
        return dev(to, z, c)

    def along_z(to):
        return dev(y, to, c)

    def pre_part(to, h):
        lhs = rows_of(x_buf[to, pl.ds(4 * h, 4)])
        return jnp.dot(lhs, rows_of(w1[...]), preferred_element_type=F32)

    ring_pre = (0, y, along_y, pre_part)
    rings([ring_pre])
    for h in range(2):
        hidden = gelu(ring_last(0, h, y, along_y, pre_part)).astype(BF16)
        hid_out[4 * h : 4 * h + 4] = hidden.reshape(4, 32, 384)

    def own_slot(p):
        return jnp.logical_and(y == c, p == c)

    def ha_copy(p):
        return remote(hid_out.at[p], h_buf.at[p, y], ha_send.at[p], ha_recv.at[y], dev(c, z, p))

    def ha_start(p, _):
        @pl.when(own_slot(p))
        def _():
            h_buf[p, y] = hid_out[p]

        @pl.when(jnp.logical_not(own_slot(p)))
        def _():
            ha_copy(p).start()

        return 0

    lax.fori_loop(0, N, ha_start, 0)

    def h_ready(h):
        def step(j, _):
            @pl.when(jnp.logical_or(y != c, j != c))
            def _():
                remote(hid_out.at[j], h_buf.at[c, j], ha_send.at[j], ha_recv.at[j], dev(j, z, y)).wait_recv()

            return 0

        lax.fori_loop(4 * h, 4 * h + 4, step, 0)

    sent_h, rest = gather_cols(h_buf, h_ready, hg_near, hg_relay, hg_sib, hg_recv)
    for copy in own_w2:
        copy.wait()
    rest()

    def out_part_a(to, h):
        return jnp.dot(rows_of(h_buf[pl.ds(4 * h, 4), to]), w2[0], preferred_element_type=F32)

    def out_part_b(to, h):
        return jnp.dot(rows_of(h_buf[to, pl.ds(4 * h, 4)]), w2[1], preferred_element_type=F32)

    ring_a, ring_b = (1, y, along_y, out_part_a), (2, z, along_z, out_part_b)
    rings([ring_a, ring_b])
    others = ((z, along_z), (y, along_y))

    def p_copy(j, k):
        place, neighbour = others[j]
        to = (place + k) % N
        return remote(part.at[j, to], part_in.at[j, place], p_send.at[j, k], p_recv.at[j, k], neighbour(to))

    for h in range(2):
        for j, (at, place, neighbour, own) in enumerate((ring_a, ring_b)):
            total = ring_last(at, h, place, neighbour, own).reshape(4, 32, 384)
            own_part[j, 4 * h : 4 * h + 4] = total
            part[j, 4 * h : 4 * h + 4] = total.astype(BF16)

    def p_start(k, _):
        for j in range(2):
            p_copy(j, k).start()
        return 0

    lax.fori_loop(1, N, p_start, 0)
    for j in range(2):
        place = others[j][0]

        def p_add(k, total):
            p_copy(j, k).wait_recv()
            return total + part_in[j, (place - k + N) % N].astype(F32)

        slab[:, 384 * j : 384 * (j + 1)] = lax.fori_loop(1, N, p_add, own_part[j, place])

    for j in range(N):
        fin_out[j] = slab[4 * j : 4 * j + 4, 0:768]

    def f_copy(p):
        return remote(fin_out.at[p], fin_in.at[c], f_send.at[p], f_recv.at[c], dev(p, z, y))

    def f_start(p, _):
        @pl.when(jnp.logical_and(y == c, p == y))
        def _():
            fin_in[c] = fin_out[p]

        @pl.when(jnp.logical_or(y != c, p != y))
        def _():
            f_copy(p).start()

        return 0

    lax.fori_loop(0, N, f_start, 0)

    over(1, y_copy, lambda copy: copy.wait_send())
    over(1, w_copy, lambda copy: copy.wait_send())
    over(1, z_copy, lambda copy: copy.wait_send())
    for copy in sent_x + sent_h:
        copy.wait_send()
    rings_sent([ring_pre, ring_a, ring_b])

    def p_sent(k, _):
        for j in range(2):
            p_copy(j, k).wait_send()
        return 0

    lax.fori_loop(1, N, p_sent, 0)

    def plane_sent(p, _):
        @pl.when(jnp.logical_or(y != c, p != c))
        def _():
            ha_copy(p).wait_send()
            f_copy(p).wait_send()
            remote(fin_out.at[p], fin_in.at[p], f_send.at[p], f_recv.at[p], dev(c, z, p)).wait_recv()

        return 0

    lax.fori_loop(0, N, plane_sent, 0)
    for j in range(N):
        cols = slice(768 * j, 768 * (j + 1))
        out_ref[:, cols] = (tok_ref[:, cols].astype(F32) + fin_in[j]).astype(BF16)


def body(tokens, norm_gain, in_weight, out_weight):
    dma = pltpu.SemaphoreType.DMA
    vmem = pl.BlockSpec(memory_space=pltpu.VMEM)
    return pl.pallas_call(
        kernel,
        out_shape=jax.ShapeDtypeStruct(tokens.shape, BF16),
        in_specs=[vmem, vmem, pl.BlockSpec(memory_space=pl.ANY), pl.BlockSpec(memory_space=pl.ANY)],
        out_specs=vmem,
        scratch_shapes=[
            pltpu.VMEM((N, 96, 384), BF16),
            pltpu.VMEM((2, 384, 384), BF16),
            pltpu.VMEM((N, 4, 768), BF16),
            pltpu.VMEM((N, 4, 768), BF16),
            pltpu.VMEM((32, 768), F32),
            pltpu.VMEM((N, N, 32, 768), BF16),
            pltpu.VMEM((N, 32, 384), BF16),
            pltpu.VMEM((N, N, 32, 384), BF16),
            pltpu.VMEM((3, 4, 4, 128, 384), BF16),
            pltpu.VMEM((3, 4, 4, 128, 384), BF16),
            pltpu.VMEM((2, N, 32, 384), BF16),
            pltpu.VMEM((2, N, 32, 384), BF16),
            pltpu.VMEM((2, N, 32, 384), F32),
            pltpu.VMEM((N, 4, 768), F32),
            pltpu.VMEM((N, 4, 768), F32),
            dma((3,)),
            dma((N,)), dma((N,)), dma((N,)), dma((N,)), dma((N,)), dma((N,)),
            dma((2, 2)), dma((2,)), dma((4, 2)), dma((N, 2)),
            dma((2, 2)), dma((2,)), dma((4, 2)), dma((N, 2)),
            dma((N,)), dma((N,)),
            dma((3, 4, 4)), dma((3, 4, 4)),
            dma((2, N)), dma((2, N)),
            dma((N,)), dma((N,)),
        ],
        compiler_params=pltpu.CompilerParams(
            collective_id=0, has_side_effects=True, vmem_limit_bytes=48 * 1024 * 1024
        ),
        cost_estimate=pl.CostEstimate(flops=2_500_000_000, bytes_accessed=1_300_000, transcendentals=100_000),
    )(tokens, norm_gain.reshape(1, -1), in_weight, out_weight)


def solution(mesh):
    return jax.shard_map(
        body,
        mesh=mesh,
        in_specs=(P(("row", "col"), None), P(), P("row", "col"), P("row", "col")),
        out_specs=P(("row", "col"), None),
        check_vma=False,
    )
```

```python
import jax
import jax.numpy as jnp
from jax import lax
from jax.experimental import pallas as pl
from jax.experimental.pallas import tpu as pltpu
from jax.sharding import PartitionSpec as P

MESH = pl.DeviceIdType.MESH
N = 8
BF16 = jnp.bfloat16
F32 = jnp.float32


def gelu(v):
    return 0.5 * v * (1.0 + jnp.tanh(0.7978845608028654 * (v + 0.044715 * (v * v * v))))


def rows_of(block):
    return block.reshape(block.shape[0] * block.shape[1], block.shape[2])


def kernel(
    tok_hbm, gain_hbm, inw_ref, outw_ref, out_ref,
    tok_ref, gain_ref, w1, w2, norm_out, norm_in, slab, x_buf, hid_out, hid_in, h_buf,
    ring_send, ring_recv, part, part_in, own_part, fin_out, fin_in,
    w_sem, y_send, y_recv, w_send, w_recv, xz_send, xg_send, xg_recv, hg_send, hg_recv,
    hc_send, hc_recv, hy_send, rs_send, rs_recv, p_send, p_recv, f_send, f_recv,
):
    row, c = lax.axis_index("row"), lax.axis_index("col")
    y, z = row // N, row % N
    x, core = c // 2, c % 2

    def dev(y_at, z_at, c_at):
        return (y_at * N + z_at, c_at)

    def col_of(x_at, core_at):
        return ((x_at + 8) % 4) * 2 + core_at

    def remote(src, dst, send, recv, target):
        return pltpu.make_async_remote_copy(
            src_ref=src, dst_ref=dst, send_sem=send, recv_sem=recv, device_id=target, device_id_type=MESH
        )

    right, left, across, sibling = col_of(x + 1, core), col_of(x - 1, core), col_of(x + 2, core), col_of(x, 1 - core)

    barrier = pltpu.get_barrier_semaphore()

    def greet(target):
        pl.semaphore_signal(barrier, inc=1, device_id=target, device_id_type=MESH)

    def greet_line(k, _):
        greet(dev((y + k) % N, z, c))
        greet(dev(y, (z + k) % N, c))
        greet(dev(y, z, (c + k) % N))
        return 0

    def greet_plane(p, _):
        @pl.when(jnp.logical_or(y != c, p != c))
        def _():
            greet(dev(c, z, p))
            greet(dev(p, z, y))

        return 0

    lax.fori_loop(1, N, greet_line, 0)
    lax.fori_loop(0, N, greet_plane, 0)

    tok_in = pltpu.make_async_copy(tok_hbm, tok_ref, w_sem.at[3])
    gain_in = pltpu.make_async_copy(gain_hbm, gain_ref, w_sem.at[4])
    tok_in.start()
    gain_in.start()
    own_w1 = pltpu.make_async_copy(inw_ref.at[:, pl.ds(pl.multiple_of(z * 384, 384), 384)], w1.at[z], w_sem.at[0])
    own_w1.start()
    own_w2 = [
        pltpu.make_async_copy(outw_ref.at[:, pl.ds(384 * j, 384)], w2.at[j], w_sem.at[1 + j]) for j in range(2)
    ]
    for copy in own_w2:
        copy.start()

    tok_in.wait()
    gain_in.wait()
    values = tok_ref[...].astype(F32)
    center = jnp.mean(values, axis=1, keepdims=True)
    spread = jnp.mean(jnp.square(values - center), axis=1, keepdims=True)
    normed = ((values - center) / jnp.sqrt(spread + 1e-06) * gain_ref[...]).astype(BF16)
    for j in range(N):
        norm_out[j] = normed[:, 768 * j : 768 * (j + 1)]
    norm_in[pl.ds(y, 1)] = norm_out[pl.ds(y, 1)]

    @pl.when(y == c)
    def _():
        pl.semaphore_wait(barrier, 35)

    @pl.when(y != c)
    def _():
        pl.semaphore_wait(barrier, 37)

    def y_copy(k):
        to = (y + k) % N
        return remote(norm_out.at[to], norm_in.at[y], y_send.at[k], y_recv.at[k], dev(to, z, c))

    def w_copy(k):
        to = (z + k) % N
        return remote(
            inw_ref.at[:, pl.ds(pl.multiple_of(to * 384, 384), 384)], w1.at[z], w_send.at[k], w_recv.at[k], dev(y, to, c)
        )

    def over(start, make, act):
        def step(k, _):
            act(make(k))
            return 0

        lax.fori_loop(start, N, step, 0)

    over(1, y_copy, lambda copy: copy.start())
    for k in (1, 7, 2, 6):
        w_copy(k).start()
    over(1, y_copy, lambda copy: copy.wait_recv())
    for j in range(N):
        slab[4 * j : 4 * j + 4, 0:768] = norm_in[j].astype(F32)
    x_buf[c, z] = slab[:, 0:768].astype(BF16)

    def offset(j):
        return jnp.where(j % 2 == 1, (j + 1) // 2, -(j // 2))

    ups = 4 - core

    def xz_copy(up, s):
        at = (z - s + N) % N if up else (z + s) % N
        to = (z + 1) % N if up else (z + N - 1) % N
        return remote(x_buf.at[c, at], x_buf.at[c, at], xz_send.at[1 - up, s], xg_recv.at[c, at], dev(y, to, c))

    def x_ready(j):
        at = (z + offset(j) + N) % N

        @pl.when(j > 0)
        def _():
            remote(x_buf.at[c, at], x_buf.at[c, at], xz_send.at[0, 0], xg_recv.at[c, at], dev(y, at, c)).wait_recv()

        s = (j + 1) // 2
        for up in (1, 0):
            mine = jnp.logical_or(j == 0, j % 2 == 1 - up)

            @pl.when(jnp.logical_and(mine, s < (ups if up else 7 - ups)))
            def _():
                xz_copy(up, s).start()

    def gather_step(buf, place, send, recv, ready, i):
        def move(of, j, kind, target):
            at = (place + offset(j) + N) % N
            return remote(buf.at[of, at], buf.at[of, at], send.at[kind, j], recv.at[of, at], dev(y, z, target))

        def start(of, j, kind, target):
            move(of, j, kind, target).start()

        def arrived(of, j):
            move(of, j, 0, sibling).wait_recv()

        @pl.when(i < N)
        def _():
            ready(i)
            start(c, i, 0, right)
            start(c, i, 1, left)
            start(c, i, 2, sibling)

        @pl.when(jnp.logical_and(i >= 1, i < N + 1))
        def _():
            j = i - 1
            arrived(left, j)

            @pl.when(j % 2 == 0)
            def _():
                start(left, j, 3, right)

            start(left, j, 4, sibling)
            arrived(right, j)

            @pl.when(j % 2 == 1)
            def _():
                start(right, j, 3, left)

            start(right, j, 5, sibling)

        @pl.when(jnp.logical_and(i >= 2, i < N + 2))
        def _():
            j = i - 2
            arrived(across, j)
            start(across, j, 6, sibling)

        @pl.when(i >= 3)
        def _():
            for d in range(4):
                arrived(col_of(x + d, 1 - core), i - 3)

    def gather_sent(buf, place, send, recv):
        def step(j, _):
            for kind in range(7):
                remote(buf.at[c, j], buf.at[c, j], send.at[kind, j], recv.at[c, j], dev(y, z, sibling)).wait_send()
            return 0

        lax.fori_loop(0, N, step, 0)

    def gather_x(i, _):
        gather_step(x_buf, z, xg_send, xg_recv, x_ready, i)
        return 0

    lax.fori_loop(0, 5, gather_x, 0)
    for k in (3, 5, 4):
        w_copy(k).start()
    lax.fori_loop(5, N, gather_x, 0)
    lax.fori_loop(N, N + 3, gather_x, 0)
    own_w1.wait()
    over(1, w_copy, lambda copy: copy.wait_recv())

    def chain(q):
        h, back = q % 4, q // 4
        steps = 4 - (h + back) % 2
        return h, 1 - 2 * back, steps

    def ring_copy(at, q, s, place, neighbour):
        _, way, _ = chain(q)
        return remote(
            ring_send.at[at, q, s], ring_recv.at[at, q, s], rs_send.at[at, q, s], rs_recv.at[at, q, s],
            neighbour((place + way + N) % N),
        )

    def ring_step(at, q, s, place, neighbour, own):
        h, way, steps = chain(q)

        @pl.when(s < steps)
        def _():
            to = (place + way * (steps - s) + N) % N
            mine = own(to, h)

            @pl.when(s == 0)
            def _():
                ring_send[at, q, s] = mine.astype(BF16)

            @pl.when(s > 0)
            def _():
                before = jnp.maximum(s - 1, 0)
                ring_copy(at, q, before, place, neighbour).wait_recv()
                ring_send[at, q, s] = (mine + ring_recv[at, q, before].astype(F32)).astype(BF16)

            ring_copy(at, q, s, place, neighbour).start()

    def ring_last(at, h, place, neighbour, own):
        total = own(place, h)
        for q in (h, 4 + h):
            last = 3 - (h + q // 4) % 2
            ring_copy(at, q, last, place, neighbour).wait_recv()
            total = total + ring_recv[at, q, last].astype(F32)
        return total

    def rings(each):
        def step(i, _):
            for at, place, neighbour, own in each:
                ring_step(at, i % 8, i // 8, place, neighbour, own)
            return 0

        lax.fori_loop(0, 32, step, 0)

    def rings_sent(each):
        def step(i, _):
            for at, place, neighbour, own in each:
                q, s = i % 8, i // 8

                @pl.when(s < chain(q)[2])
                def _():
                    ring_copy(at, q, s, place, neighbour).wait_send()

            return 0

        lax.fori_loop(0, 32, step, 0)

    def along_y(to):
        return dev(to, z, c)

    def along_z(to):
        return dev(y, to, c)

    def pre_part(to, h):
        lhs = rows_of(x_buf[to, pl.ds(2 * h, 2)])
        return jnp.dot(lhs, rows_of(w1[...]), preferred_element_type=F32)

    ring_pre = (0, y, along_y, pre_part)
    rings([ring_pre])
    for h in range(4):
        hidden = gelu(ring_last(0, h, y, along_y, pre_part)).astype(BF16)
        hid_out[2 * h : 2 * h + 2] = hidden.reshape(2, 32, 384)

    def hc_copy(k):
        to = (c + k) % N
        return remote(hid_out.at[to], hid_in.at[c], hc_send.at[k], hc_recv.at[k], dev(y, z, to))

    def hy_copy(of):
        return remote(hid_in.at[of], h_buf.at[c, y], hy_send.at[of], hg_recv.at[c, y], dev(of, z, c))

    def pass_on(of):
        @pl.when(of == y)
        def _():
            h_buf[c, y] = hid_in[of]

        @pl.when(of != y)
        def _():
            hy_copy(of).start()

    over(1, hc_copy, lambda copy: copy.start())
    hid_in[pl.ds(c, 1)] = hid_out[pl.ds(c, 1)]
    pass_on(c)

    def hc_arrived(k, _):
        hc_copy(k).wait_recv()
        pass_on((c - k + N) % N)
        return 0

    lax.fori_loop(1, N, hc_arrived, 0)

    def h_ready(j):
        at = (y + offset(j) + N) % N

        @pl.when(j > 0)
        def _():
            remote(h_buf.at[c, at], h_buf.at[c, at], hy_send.at[0], hg_recv.at[c, at], dev(at, z, c)).wait_recv()

    def gather_h(i, _):
        gather_step(h_buf, y, hg_send, hg_recv, h_ready, i)
        return 0

    for copy in own_w2:
        copy.wait()
    lax.fori_loop(0, N, gather_h, 0)
    lax.fori_loop(N, N + 3, gather_h, 0)

    def out_part_a(to, h):
        return jnp.dot(rows_of(h_buf[pl.ds(2 * h, 2), to]), w2[0], preferred_element_type=F32)

    def out_part_b(to, h):
        return jnp.dot(rows_of(h_buf[to, pl.ds(2 * h, 2)]), w2[1], preferred_element_type=F32)

    ring_a, ring_b = (1, y, along_y, out_part_a), (2, z, along_z, out_part_b)
    rings([ring_a, ring_b])
    others = ((z, along_z), (y, along_y))

    def p_copy(j, k):
        place, neighbour = others[j]
        to = (place + k) % N
        return remote(part.at[j, to], part_in.at[j, place], p_send.at[j, k], p_recv.at[j, k], neighbour(to))

    for h in range(4):
        for j, (at, place, neighbour, own) in enumerate((ring_a, ring_b)):
            total = ring_last(at, h, place, neighbour, own).reshape(2, 32, 384)
            own_part[j, 2 * h : 2 * h + 2] = total
            part[j, 2 * h : 2 * h + 2] = total.astype(BF16)

    def p_start(k, _):
        for j in range(2):
            p_copy(j, k).start()
        return 0

    lax.fori_loop(1, N, p_start, 0)
    for j in range(2):
        place = others[j][0]

        def p_add(k, total):
            p_copy(j, k).wait_recv()
            return total + part_in[j, (place - k + N) % N].astype(F32)

        slab[:, 384 * j : 384 * (j + 1)] = lax.fori_loop(1, N, p_add, own_part[j, place])

    for j in range(N):
        fin_out[j] = slab[4 * j : 4 * j + 4, 0:768]

    def f_copy(p):
        return remote(fin_out.at[p], fin_in.at[c], f_send.at[p], f_recv.at[c], dev(p, z, y))

    def f_start(p, _):
        @pl.when(jnp.logical_and(y == c, p == y))
        def _():
            fin_in[c] = fin_out[p]

        @pl.when(jnp.logical_or(y != c, p != y))
        def _():
            f_copy(p).start()

        return 0

    lax.fori_loop(0, N, f_start, 0)

    over(1, y_copy, lambda copy: copy.wait_send())
    over(1, w_copy, lambda copy: copy.wait_send())
    over(1, hc_copy, lambda copy: copy.wait_send())
    gather_sent(x_buf, z, xg_send, xg_recv)
    gather_sent(h_buf, y, hg_send, hg_recv)
    for up in (1, 0):
        for s in range(4):

            @pl.when(s < (ups if up else 7 - ups))
            def _():
                xz_copy(up, s).wait_send()

    def hy_sent(of, _):
        @pl.when(of != y)
        def _():
            hy_copy(of).wait_send()

        return 0

    lax.fori_loop(0, N, hy_sent, 0)
    rings_sent([ring_pre, ring_a, ring_b])

    def p_sent(k, _):
        for j in range(2):
            p_copy(j, k).wait_send()
        return 0

    lax.fori_loop(1, N, p_sent, 0)

    def plane_sent(p, _):
        @pl.when(jnp.logical_or(y != c, p != c))
        def _():
            f_copy(p).wait_send()
            remote(fin_out.at[p], fin_in.at[p], f_send.at[p], f_recv.at[p], dev(c, z, p)).wait_recv()

        return 0

    lax.fori_loop(0, N, plane_sent, 0)
    for j in range(N):
        cols = slice(768 * j, 768 * (j + 1))
        out_ref[:, cols] = (tok_ref[:, cols].astype(F32) + fin_in[j]).astype(BF16)


def body(tokens, norm_gain, in_weight, out_weight):
    dma = pltpu.SemaphoreType.DMA
    return pl.pallas_call(
        kernel,
        out_shape=jax.ShapeDtypeStruct(tokens.shape, BF16),
        in_specs=[pl.BlockSpec(memory_space=pltpu.HBM)] * 4,
        out_specs=pl.BlockSpec(memory_space=pltpu.VMEM),
        scratch_shapes=[
            pltpu.VMEM((4, 6144), BF16),
            pltpu.VMEM((1, 6144), F32),
            pltpu.VMEM((N, 96, 384), BF16),
            pltpu.VMEM((2, 384, 384), BF16),
            pltpu.VMEM((N, 4, 768), BF16),
            pltpu.VMEM((N, 4, 768), BF16),
            pltpu.VMEM((32, 768), F32),
            pltpu.VMEM((N, N, 32, 768), BF16),
            pltpu.VMEM((N, 32, 384), BF16),
            pltpu.VMEM((N, 32, 384), BF16),
            pltpu.VMEM((N, N, 32, 384), BF16),
            pltpu.VMEM((3, 8, 4, 64, 384), BF16),
            pltpu.VMEM((3, 8, 4, 64, 384), BF16),
            pltpu.VMEM((2, N, 32, 384), BF16),
            pltpu.VMEM((2, N, 32, 384), BF16),
            pltpu.VMEM((2, N, 32, 384), F32),
            pltpu.VMEM((N, 4, 768), F32),
            pltpu.VMEM((N, 4, 768), F32),
            dma((5,)),
            dma((N,)), dma((N,)), dma((N,)), dma((N,)),
            dma((2, 4)), dma((7, N)), dma((N, N)), dma((7, N)), dma((N, N)),
            dma((N,)), dma((N,)), dma((N,)),
            dma((3, 8, 4)), dma((3, 8, 4)),
            dma((2, N)), dma((2, N)),
            dma((N,)), dma((N,)),
        ],
        compiler_params=pltpu.CompilerParams(
            collective_id=0, has_side_effects=True, vmem_limit_bytes=62 * 1024 * 1024
        ),
        cost_estimate=pl.CostEstimate(flops=2_500_000_000, bytes_accessed=1_300_000, transcendentals=100_000),
    )(tokens, norm_gain.reshape(1, -1), in_weight, out_weight)


def solution(mesh):
    return jax.shard_map(
        body,
        mesh=mesh,
        in_specs=(P(("row", "col"), None), P(), P("row", "col"), P("row", "col")),
        out_specs=P(("row", "col"), None),
        check_vma=False,
    )
```

```python
import jax
import jax.numpy as jnp
from jax import lax
from jax.experimental import pallas as pl
from jax.experimental.pallas import tpu as pltpu
from jax.sharding import PartitionSpec as P

MESH = pl.DeviceIdType.MESH
N = 8
BF16 = jnp.bfloat16
F32 = jnp.float32


def gelu(v):
    return 0.5 * v * (1.0 + jnp.tanh(0.7978845608028654 * (v + 0.044715 * (v * v * v))))


def rows_of(block):
    return block.reshape(block.shape[0] * block.shape[1], block.shape[2])


def kernel(
    tok_hbm, gain_hbm, inw_ref, outw_ref, out_ref,
    tok_ref, gain_ref, w1, w2, norm_out, norm_in, slab, x_buf, hid_out, hid_in, h_buf,
    ring_send, ring_recv, part, part_in, own_part, fin_out, fin_in,
    w_sem, y_send, y_recv, w_send, w_recv, xz_send, xg_send, xg_recv, hg_send, hg_recv,
    hc_send, hc_recv, hy_send, rs_send, rs_recv, p_send, p_recv, f_send, f_recv,
):
    row, c = lax.axis_index("row"), lax.axis_index("col")
    y, z = row // N, row % N
    x, core = c // 2, c % 2

    def dev(y_at, z_at, c_at):
        return (y_at * N + z_at, c_at)

    def col_of(x_at, core_at):
        return ((x_at + 8) % 4) * 2 + core_at

    def remote(src, dst, send, recv, target):
        return pltpu.make_async_remote_copy(
            src_ref=src, dst_ref=dst, send_sem=send, recv_sem=recv, device_id=target, device_id_type=MESH
        )

    right, left, across, sibling = col_of(x + 1, core), col_of(x - 1, core), col_of(x + 2, core), col_of(x, 1 - core)

    barrier = pltpu.get_barrier_semaphore()

    def greet(target):
        pl.semaphore_signal(barrier, inc=1, device_id=target, device_id_type=MESH)

    def greet_line(k, _):
        greet(dev((y + k) % N, z, c))
        greet(dev(y, (z + k) % N, c))
        greet(dev(y, z, (c + k) % N))
        return 0

    def greet_plane(p, _):
        @pl.when(jnp.logical_or(y != c, p != c))
        def _():
            greet(dev(c, z, p))
            greet(dev(p, z, y))

        return 0

    lax.fori_loop(1, N, greet_line, 0)
    lax.fori_loop(0, N, greet_plane, 0)

    tok_in = pltpu.make_async_copy(tok_hbm, tok_ref, w_sem.at[3])
    gain_in = pltpu.make_async_copy(gain_hbm, gain_ref, w_sem.at[4])
    tok_in.start()
    gain_in.start()
    own_w1 = pltpu.make_async_copy(inw_ref.at[:, pl.ds(pl.multiple_of(z * 384, 384), 384)], w1.at[z], w_sem.at[0])
    own_w1.start()
    own_w2 = [
        pltpu.make_async_copy(outw_ref.at[:, pl.ds(384 * j, 384)], w2.at[j], w_sem.at[1 + j]) for j in range(2)
    ]
    for copy in own_w2:
        copy.start()

    tok_in.wait()
    gain_in.wait()
    values = tok_ref[...].astype(F32)
    center = jnp.mean(values, axis=1, keepdims=True)
    spread = jnp.mean(jnp.square(values - center), axis=1, keepdims=True)
    normed = ((values - center) / jnp.sqrt(spread + 1e-06) * gain_ref[...]).astype(BF16)
    for j in range(N):
        norm_out[j] = normed[:, 768 * j : 768 * (j + 1)]
    norm_in[pl.ds(y, 1)] = norm_out[pl.ds(y, 1)]

    @pl.when(y == c)
    def _():
        pl.semaphore_wait(barrier, 35)

    @pl.when(y != c)
    def _():
        pl.semaphore_wait(barrier, 37)

    def y_copy(k):
        to = (y + k) % N
        return remote(norm_out.at[to], norm_in.at[y], y_send.at[k], y_recv.at[k], dev(to, z, c))

    def w_copy(k):
        to = (z + k) % N
        return remote(
            inw_ref.at[:, pl.ds(pl.multiple_of(to * 384, 384), 384)], w1.at[z], w_send.at[k], w_recv.at[k], dev(y, to, c)
        )

    def over(start, make, act):
        def step(k, _):
            act(make(k))
            return 0

        lax.fori_loop(start, N, step, 0)

    over(1, y_copy, lambda copy: copy.start())
    for k in (1, 7, 2, 6):
        w_copy(k).start()
    over(1, y_copy, lambda copy: copy.wait_recv())
    for j in range(N):
        slab[4 * j : 4 * j + 4, 0:768] = norm_in[j].astype(F32)
    x_buf[c, z] = slab[:, 0:768].astype(BF16)

    def offset(j):
        return jnp.where(j % 2 == 1, (j + 1) // 2, -(j // 2))

    def xz_copy(kind, at, shift):
        at, to = (z + at + N) % N, (z + shift + N) % N
        return remote(x_buf.at[c, at], x_buf.at[c, at], xz_send.at[kind], xg_recv.at[c, at], dev(y, to, c))

    xz_own = [xz_copy(0, 0, 2), xz_copy(1, 0, -2), xz_copy(2, 0, 1), xz_copy(3, 0, -1)]
    xz_near = [xz_copy(4, 2, -1), xz_copy(5, -2, 1)]

    def xz_far(act):
        @pl.when(core == 0)
        def _():
            act(xz_copy(6, -2, 2))

        @pl.when(core == 1)
        def _():
            act(xz_copy(6, 2, -2))

    for copy in xz_own:
        copy.start()

    def x_ready(j):
        at = (z + offset(j) + N) % N

        @pl.when(j > 0)
        def _():
            remote(x_buf.at[c, at], x_buf.at[c, at], xz_send.at[0], xg_recv.at[c, at], dev(y, at, c)).wait_recv()

        @pl.when(j == 4)
        def _():
            xz_near[0].start()
            xz_near[1].start()
            xz_far(lambda copy: copy.start())

    def gather(buf, place, send, recv, ready, between=None):
        def move(of, j, kind, target):
            at = (place + offset(j) + N) % N
            return remote(buf.at[of, at], buf.at[of, at], send.at[kind, j], recv.at[of, at], dev(y, z, target))

        def start(of, j, kind, target):
            move(of, j, kind, target).start()

        def arrived(of, j):
            move(of, j, 0, sibling).wait_recv()

        def own_step(j, _):
            ready(j)
            start(c, j, 0, right)
            start(c, j, 1, left)
            start(c, j, 2, sibling)
            return 0

        def near_step(j, _):
            arrived(left, j)

            @pl.when(j % 2 == 0)
            def _():
                start(left, j, 3, right)

            start(left, j, 4, sibling)
            arrived(right, j)

            @pl.when(j % 2 == 1)
            def _():
                start(right, j, 3, left)

            start(right, j, 5, sibling)
            return 0

        def far_step(j, _):
            arrived(across, j)
            start(across, j, 6, sibling)
            return 0

        def rest_step(j, _):
            for d in range(4):
                arrived(col_of(x + d, 1 - core), j)
            return 0

        lax.fori_loop(0, N, own_step, 0)
        if between is not None:
            between()
        for step in (near_step, far_step, rest_step):
            lax.fori_loop(0, N, step, 0)

    def gather_sent(buf, place, send, recv):
        def step(j, _):
            for kind in range(7):
                remote(buf.at[c, j], buf.at[c, j], send.at[kind, j], recv.at[c, j], dev(y, z, sibling)).wait_send()
            return 0

        lax.fori_loop(0, N, step, 0)

    def rest_of_w():
        for k in (3, 5, 4):
            w_copy(k).start()

    gather(x_buf, z, xg_send, xg_recv, x_ready, rest_of_w)
    own_w1.wait()
    over(1, w_copy, lambda copy: copy.wait_recv())

    def chain(q):
        h, back = q % 4, q // 4
        steps = 4 - (h + back) % 2
        return h, 1 - 2 * back, steps

    def ring_copy(at, q, s, place, neighbour):
        _, way, _ = chain(q)
        return remote(
            ring_send.at[at, q, s], ring_recv.at[at, q, s], rs_send.at[at, q, s], rs_recv.at[at, q, s],
            neighbour((place + way + N) % N),
        )

    def ring_step(at, q, s, place, neighbour, own):
        h, way, steps = chain(q)

        @pl.when(s < steps)
        def _():
            to = (place + way * (steps - s) + N) % N
            mine = own(to, h)

            @pl.when(s == 0)
            def _():
                ring_send[at, q, s] = mine.astype(BF16)

            @pl.when(s > 0)
            def _():
                before = jnp.maximum(s - 1, 0)
                ring_copy(at, q, before, place, neighbour).wait_recv()
                ring_send[at, q, s] = (mine + ring_recv[at, q, before].astype(F32)).astype(BF16)

            ring_copy(at, q, s, place, neighbour).start()

    def ring_last(at, h, place, neighbour, own):
        total = own(place, h)
        for q in (h, 4 + h):
            last = 3 - (h + q // 4) % 2
            ring_copy(at, q, last, place, neighbour).wait_recv()
            total = total + ring_recv[at, q, last].astype(F32)
        return total

    def rings(each):
        def step(i, _):
            for at, place, neighbour, own in each:
                ring_step(at, i % 8, i // 8, place, neighbour, own)
            return 0

        lax.fori_loop(0, 32, step, 0)

    def rings_sent(each):
        def step(i, _):
            for at, place, neighbour, own in each:
                q, s = i % 8, i // 8

                @pl.when(s < chain(q)[2])
                def _():
                    ring_copy(at, q, s, place, neighbour).wait_send()

            return 0

        lax.fori_loop(0, 32, step, 0)

    def along_y(to):
        return dev(to, z, c)

    def along_z(to):
        return dev(y, to, c)

    def pre_part(to, h):
        lhs = rows_of(x_buf[to, pl.ds(2 * h, 2)])
        return jnp.dot(lhs, rows_of(w1[...]), preferred_element_type=F32)

    ring_pre = (0, y, along_y, pre_part)
    rings([ring_pre])
    for h in range(4):
        hidden = gelu(ring_last(0, h, y, along_y, pre_part)).astype(BF16)
        hid_out[2 * h : 2 * h + 2] = hidden.reshape(2, 32, 384)

    def hc_copy(k):
        to = (c + k) % N
        return remote(hid_out.at[to], hid_in.at[c], hc_send.at[k], hc_recv.at[k], dev(y, z, to))

    def hy_copy(of):
        return remote(hid_in.at[of], h_buf.at[c, y], hy_send.at[of], hg_recv.at[c, y], dev(of, z, c))

    def pass_on(of):
        @pl.when(of == y)
        def _():
            h_buf[c, y] = hid_in[of]

        @pl.when(of != y)
        def _():
            hy_copy(of).start()

    over(1, hc_copy, lambda copy: copy.start())
    hid_in[pl.ds(c, 1)] = hid_out[pl.ds(c, 1)]
    pass_on(c)

    def hc_arrived(k, _):
        hc_copy(k).wait_recv()
        pass_on((c - k + N) % N)
        return 0

    lax.fori_loop(1, N, hc_arrived, 0)

    def h_ready(j):
        at = (y + offset(j) + N) % N

        @pl.when(j > 0)
        def _():
            remote(h_buf.at[c, at], h_buf.at[c, at], hy_send.at[0], hg_recv.at[c, at], dev(at, z, c)).wait_recv()

    for copy in own_w2:
        copy.wait()
    gather(h_buf, y, hg_send, hg_recv, h_ready)

    def out_part_a(to, h):
        return jnp.dot(rows_of(h_buf[pl.ds(2 * h, 2), to]), w2[0], preferred_element_type=F32)

    def out_part_b(to, h):
        return jnp.dot(rows_of(h_buf[to, pl.ds(2 * h, 2)]), w2[1], preferred_element_type=F32)

    ring_a, ring_b = (1, y, along_y, out_part_a), (2, z, along_z, out_part_b)
    rings([ring_a, ring_b])
    others = ((z, along_z), (y, along_y))

    def p_copy(j, k):
        place, neighbour = others[j]
        to = (place + k) % N
        return remote(part.at[j, to], part_in.at[j, place], p_send.at[j, k], p_recv.at[j, k], neighbour(to))

    for h in range(4):
        for j, (at, place, neighbour, own) in enumerate((ring_a, ring_b)):
            total = ring_last(at, h, place, neighbour, own).reshape(2, 32, 384)
            own_part[j, 2 * h : 2 * h + 2] = total
            part[j, 2 * h : 2 * h + 2] = total.astype(BF16)

    def p_start(k, _):
        for j in range(2):
            p_copy(j, k).start()
        return 0

    lax.fori_loop(1, N, p_start, 0)
    for j in range(2):
        place = others[j][0]

        def p_add(k, total):
            p_copy(j, k).wait_recv()
            return total + part_in[j, (place - k + N) % N].astype(F32)

        slab[:, 384 * j : 384 * (j + 1)] = lax.fori_loop(1, N, p_add, own_part[j, place])

    for j in range(N):
        fin_out[j] = slab[4 * j : 4 * j + 4, 0:768]

    def f_copy(p):
        return remote(fin_out.at[p], fin_in.at[c], f_send.at[p], f_recv.at[c], dev(p, z, y))

    def f_start(p, _):
        @pl.when(jnp.logical_and(y == c, p == y))
        def _():
            fin_in[c] = fin_out[p]

        @pl.when(jnp.logical_or(y != c, p != y))
        def _():
            f_copy(p).start()

        return 0

    lax.fori_loop(0, N, f_start, 0)

    over(1, y_copy, lambda copy: copy.wait_send())
    over(1, w_copy, lambda copy: copy.wait_send())
    over(1, hc_copy, lambda copy: copy.wait_send())
    gather_sent(x_buf, z, xg_send, xg_recv)
    gather_sent(h_buf, y, hg_send, hg_recv)
    for copy in xz_own + xz_near:
        copy.wait_send()
    xz_far(lambda copy: copy.wait_send())

    def hy_sent(of, _):
        @pl.when(of != y)
        def _():
            hy_copy(of).wait_send()

        return 0

    lax.fori_loop(0, N, hy_sent, 0)
    rings_sent([ring_pre, ring_a, ring_b])

    def p_sent(k, _):
        for j in range(2):
            p_copy(j, k).wait_send()
        return 0

    lax.fori_loop(1, N, p_sent, 0)

    def plane_sent(p, _):
        @pl.when(jnp.logical_or(y != c, p != c))
        def _():
            f_copy(p).wait_send()
            remote(fin_out.at[p], fin_in.at[p], f_send.at[p], f_recv.at[p], dev(c, z, p)).wait_recv()

        return 0

    lax.fori_loop(0, N, plane_sent, 0)
    for j in range(N):
        cols = slice(768 * j, 768 * (j + 1))
        out_ref[:, cols] = (tok_ref[:, cols].astype(F32) + fin_in[j]).astype(BF16)


def body(tokens, norm_gain, in_weight, out_weight):
    dma = pltpu.SemaphoreType.DMA
    return pl.pallas_call(
        kernel,
        out_shape=jax.ShapeDtypeStruct(tokens.shape, BF16),
        in_specs=[pl.BlockSpec(memory_space=pltpu.HBM)] * 4,
        out_specs=pl.BlockSpec(memory_space=pltpu.VMEM),
        scratch_shapes=[
            pltpu.VMEM((4, 6144), BF16),
            pltpu.VMEM((1, 6144), F32),
            pltpu.VMEM((N, 96, 384), BF16),
            pltpu.VMEM((2, 384, 384), BF16),
            pltpu.VMEM((N, 4, 768), BF16),
            pltpu.VMEM((N, 4, 768), BF16),
            pltpu.VMEM((32, 768), F32),
            pltpu.VMEM((N, N, 32, 768), BF16),
            pltpu.VMEM((N, 32, 384), BF16),
            pltpu.VMEM((N, 32, 384), BF16),
            pltpu.VMEM((N, N, 32, 384), BF16),
            pltpu.VMEM((3, 8, 4, 64, 384), BF16),
            pltpu.VMEM((3, 8, 4, 64, 384), BF16),
            pltpu.VMEM((2, N, 32, 384), BF16),
            pltpu.VMEM((2, N, 32, 384), BF16),
            pltpu.VMEM((2, N, 32, 384), F32),
            pltpu.VMEM((N, 4, 768), F32),
            pltpu.VMEM((N, 4, 768), F32),
            dma((5,)),
            dma((N,)), dma((N,)), dma((N,)), dma((N,)),
            dma((7,)), dma((7, N)), dma((N, N)), dma((7, N)), dma((N, N)),
            dma((N,)), dma((N,)), dma((N,)),
            dma((3, 8, 4)), dma((3, 8, 4)),
            dma((2, N)), dma((2, N)),
            dma((N,)), dma((N,)),
        ],
        compiler_params=pltpu.CompilerParams(
            collective_id=0, has_side_effects=True, vmem_limit_bytes=62 * 1024 * 1024
        ),
        cost_estimate=pl.CostEstimate(flops=2_500_000_000, bytes_accessed=1_300_000, transcendentals=100_000),
    )(tokens, norm_gain.reshape(1, -1), in_weight, out_weight)


def solution(mesh):
    return jax.shard_map(
        body,
        mesh=mesh,
        in_specs=(P(("row", "col"), None), P(), P("row", "col"), P("row", "col")),
        out_specs=P(("row", "col"), None),
        check_vma=False,
    )
```

```python
import jax
import jax.numpy as jnp
from jax import lax
from jax.experimental import pallas as pl
from jax.experimental.pallas import tpu as pltpu
from jax.sharding import PartitionSpec as P

MESH = pl.DeviceIdType.MESH
N = 8
BF16 = jnp.bfloat16
F32 = jnp.float32


def gelu(v):
    return 0.5 * v * (1.0 + jnp.tanh(0.7978845608028654 * (v + 0.044715 * (v * v * v))))


def rows_of(block):
    return block.reshape(-1, block.shape[-1])


S_Y, S_W, S_Z, S_X, S_H, S_R, S_HC, S_HY, S_P, S_F, SENDS = 0, 1, 2, 3, 5, 7, 10, 11, 12, 13, 14


def kernel(
    tok_hbm, gain_hbm, inw_ref, outw_ref, out_ref,
    tok_ref, gain_ref, w1, w2, norm_out, norm_in, slab, x_buf, pre_own, hid_out, hid_in, h_buf, out_own,
    ring_send, ring_recv, part, part_in, own_part, fin_out, fin_in,
    w_sem, sent, y_recv, w_recv, z_recv, x_recv, h_recv, hc_recv, hy_recv, rs_recv, p_recv, f_recv,
):
    row, c = lax.axis_index("row"), lax.axis_index("col")
    y, z = row // N, row % N
    x, core = c // 2, c % 2

    def dev(y_at, z_at, c_at):
        return (y_at * N + z_at, c_at)

    def col_of(x_at, core_at):
        return ((x_at + 8) % 4) * 2 + core_at

    right, left, across, sibling = col_of(x + 1, core), col_of(x - 1, core), col_of(x + 2, core), col_of(x, 1 - core)

    def remote(src, dst, kind, recv, target):
        return pltpu.make_async_remote_copy(
            src_ref=src, dst_ref=dst, send_sem=sent.at[kind], recv_sem=recv, device_id=target, device_id_type=MESH
        )

    def take(ref, recv):
        remote(ref, ref, S_Y, recv, dev(y, z, sibling)).wait_recv()

    def drain(ref, kind):
        remote(ref, ref, kind, f_recv, dev(y, z, sibling)).wait_send()

    def loop(start, end, act):
        def step(k, _):
            act(k)
            return 0

        lax.fori_loop(start, end, step, 0)

    tok_in = pltpu.make_async_copy(tok_hbm, tok_ref, w_sem.at[2])
    gain_in = pltpu.make_async_copy(gain_hbm, gain_ref, w_sem.at[3])
    tok_in.start()
    gain_in.start()

    barrier = pltpu.get_barrier_semaphore()

    def greet(target):
        pl.semaphore_signal(barrier, inc=1, device_id=target, device_id_type=MESH)

    def greet_line(k):
        greet(dev((y + k) % N, z, c))
        greet(dev(y, (z + k) % N, c))
        greet(dev(y, z, (c + k) % N))

    def greet_plane(p):
        @pl.when(jnp.logical_or(y != c, p != c))
        def _():
            greet(dev(c, z, p))
            greet(dev(p, z, y))

    loop(1, N, greet_line)
    loop(0, N, greet_plane)

    own_w1 = pltpu.make_async_copy(inw_ref.at[:, pl.ds(pl.multiple_of(z * 384, 384), 384)], w1.at[z], w_sem.at[0])
    own_w2 = pltpu.make_async_copy(outw_ref, w2, w_sem.at[1])
    own_w1.start()
    own_w2.start()

    tok_in.wait()
    gain_in.wait()
    values = tok_ref[...].astype(F32)
    center = jnp.mean(values, axis=1, keepdims=True)
    spread = jnp.mean(jnp.square(values - center), axis=1, keepdims=True)
    normed = ((values - center) / jnp.sqrt(spread + 1e-06) * gain_ref[...]).astype(BF16)
    for j in range(N):
        norm_out[j] = normed[:, 768 * j : 768 * (j + 1)]
    norm_in[pl.ds(y, 1)] = norm_out[pl.ds(y, 1)]

    @pl.when(y == c)
    def _():
        pl.semaphore_wait(barrier, 35)

    @pl.when(y != c)
    def _():
        pl.semaphore_wait(barrier, 37)

    def y_start(k):
        to = (y + k) % N
        remote(norm_out.at[to], norm_in.at[y], S_Y, y_recv, dev(to, z, c)).start()

    def w_start(k):
        to = (z + k) % N
        remote(
            inw_ref.at[:, pl.ds(pl.multiple_of(to * 384, 384), 384)], w1.at[z], S_W, w_recv, dev(y, to, c)
        ).start()

    loop(1, N, y_start)
    for k in (1, 7):
        w_start(k)
    take(norm_in.at[0:7], y_recv)
    for j in range(N):
        slab[4 * j : 4 * j + 4] = norm_in[j].astype(F32)
    for hf in range(2):
        x_buf[hf, c, z] = slab[16 * hf : 16 * hf + 16].astype(BF16)

    def z_copy(at, shift):
        at, to = (z + at + N) % N, (z + shift + N) % N
        return remote(x_buf.at[:, c, at], x_buf.at[:, c, at], S_Z, z_recv.at[at], dev(y, to, c))

    for shift in (2, -2, 1, -1):
        z_copy(0, shift).start()

    def x_own(hf):
        for off in (0, 2, -2, 1, -1, 3, -3, 4):
            at = (z + off + N) % N
            block = x_buf.at[hf, c, at]
            if hf == 0 and off != 0:
                take(x_buf.at[:, c, at], z_recv.at[at])
            if hf == 0 and off == -2:
                z_copy(2, -1).start()
                z_copy(-2, 1).start()

                @pl.when(core == 0)
                def _():
                    z_copy(-2, 2).start()

                @pl.when(core == 1)
                def _():
                    z_copy(2, -2).start()

                for k in (2, 6, 3, 5, 4):
                    w_start(k)
            remote(block, block, S_X + hf, x_recv.at[hf, at // 4], dev(y, z, right)).start()
            remote(block, block, S_X + hf, x_recv.at[hf, 2 + at // 4], dev(y, z, left)).start()
        remote(x_buf.at[hf, c], x_buf.at[hf, c], S_X + hf, x_recv.at[hf, 6], dev(y, z, sibling)).start()

    def h_own(hf):
        take(h_buf.at[hf, c, 0:7], hy_recv.at[hf])
        for g in range(2):
            block = h_buf.at[hf, c, 4 * g : 4 * g + 4]
            remote(block, block, S_H + hf, h_recv.at[hf, g], dev(y, z, right)).start()
            remote(block, block, S_H + hf, h_recv.at[hf, 2 + g], dev(y, z, left)).start()
        for g in range(2):
            block = h_buf.at[hf, c, 4 * g : 4 * g + 4]
            remote(block, block, S_H + hf, h_recv.at[hf, 4 + g], dev(y, z, across)).start()
        remote(h_buf.at[hf, c], h_buf.at[hf, c], S_H + hf, h_recv.at[hf, 6], dev(y, z, sibling)).start()

    class Gather:
        def __init__(self, buf, kind, recv):
            self.buf, self.kind, self.recv = buf, kind, recv

        def block(self, hf, of, g):
            return self.buf.at[hf, of, 4 * g : 4 * g + 4]

        def to_sibling(self, hf, of):
            block = self.buf.at[hf, of]
            remote(block, block, self.kind + hf, self.recv.at[hf, 6], dev(y, z, sibling)).start()

        def near(self, hf):
            if self.kind == S_X:
                for of, g, side, to, far in ((left, 0, 0, right, 4), (right, 1, 2, left, 5)):
                    block = self.block(hf, of, g)
                    take(block, self.recv.at[hf, side + g])
                    remote(block, block, self.kind + hf, self.recv.at[hf, far], dev(y, z, to)).start()
                self.beside(hf, ((left, 1, 0), (right, 0, 2)))
            else:
                self.beside(hf, ((left, 0, 0), (left, 1, 0)), left)
                self.beside(hf, ((right, 0, 2), (right, 1, 2)), right)

        def beside(self, hf, blocks, whole=None):
            for of, g, side in blocks:
                take(self.block(hf, of, g), self.recv.at[hf, side + g])
                if whole is None:
                    self.to_sibling(hf, of)
            if whole is not None:
                self.to_sibling(hf, whole)

        def far(self, hf):
            for g in range(2):
                take(self.block(hf, across, g), self.recv.at[hf, 4 + g])
            self.to_sibling(hf, across)

        def rest(self, hf):
            take(self.buf.at[hf, 0:4], self.recv.at[hf, 6])

    def ring_copy(at, q, s, i, place, neighbour):
        way = 1 - 2 * (i % 2)
        return remote(
            ring_send.at[at, q, s], ring_recv.at[at, q, s], S_R + at, rs_recv.at[at, q, s], neighbour((place + way + N) % N)
        )

    def rings(hf, s, each):
        def step(i):
            odd = (i % 2 + i // 2) % 2
            q = hf * 4 + i

            def act():
                for at, place, neighbour, own in each:
                    to = (place + (1 - 2 * (i % 2)) * (4 - odd - s) + N) % N
                    mine = own(hf, to, i // 2)
                    if s > 0:
                        take(ring_recv.at[at, q, s - 1], rs_recv.at[at, q, s - 1])
                        mine = mine + ring_recv[at, q, s - 1].astype(F32)
                    ring_send[at, q, s] = mine.astype(BF16)
                    ring_copy(at, q, s, i, place, neighbour).start()

            if s < 3:
                act()
            else:
                pl.when(odd == 0)(act)

        loop(0, 4, step)

    def ring_last(hf, p, ring):
        at, place, _, own = ring
        total = own(hf, place, p)
        for i in (2 * p, 2 * p + 1):
            q, s = hf * 4 + i, 3 - (p + i % 2) % 2
            take(ring_recv.at[at, q, s], rs_recv.at[at, q, s])
            total = total + ring_recv[at, q, s].astype(F32)
        return total.reshape(4, 16, 384)

    def along_y(to):
        return dev(to, z, c)

    def along_z(to):
        return dev(y, to, c)

    def pre_product(hf):
        def step(t):
            rows = rows_of(x_buf[hf, pl.ds(4 * t, 4)])
            sums = jnp.dot(rows, rows_of(w1[...]), preferred_element_type=F32)
            pre_own[hf, pl.ds(4 * t, 4)] = sums.reshape(4, N, 16, 384)

        loop(0, 2, step)

    def out_product(hf):
        def step(t):
            rows = rows_of(h_buf[hf, pl.ds(4 * t, 4)])
            sums = jnp.dot(rows, w2[...], preferred_element_type=F32)
            out_own[hf, pl.ds(4 * t, 4)] = sums.reshape(4, N, 16, 768)

        loop(0, 2, step)

    def pre_part(hf, to, p):
        return rows_of(pre_own[hf, to, pl.ds(4 * p, 4)])

    def out_part_a(hf, to, p):
        return rows_of(out_own[hf, pl.ds(4 * p, 4), to, :, 0:384])

    def out_part_b(hf, to, p):
        return rows_of(out_own[hf, to, pl.ds(4 * p, 4), :, 384:768])

    ring_pre = (0, y, along_y, pre_part)
    ring_out = ((1, y, along_y, out_part_a), (2, z, along_z, out_part_b))

    def pass_on(hf, of):
        @pl.when(of == y)
        def _():
            h_buf[hf, c, y] = hid_in[hf, of]

        @pl.when(of != y)
        def _():
            remote(hid_in.at[hf, of], h_buf.at[hf, c, y], S_HY, hy_recv.at[hf], dev(of, z, c)).start()

    def hidden(hf):
        for p in range(2):
            hid_out[hf, 4 * p : 4 * p + 4] = gelu(ring_last(hf, p, ring_pre)).astype(BF16)

        def start(k):
            to = (c + k) % N
            remote(hid_out.at[hf, to], hid_in.at[hf, c], S_HC, hc_recv.at[hf], dev(y, z, to)).start()

        loop(1, N, start)
        hid_in[hf, c] = hid_out[hf, c]
        pass_on(hf, c)

    def hidden_on(hf):
        take(hid_in.at[hf, 0:7], hc_recv.at[hf])
        loop(1, N, lambda k: pass_on(hf, (c + k) % N))

    others = ((z, along_z), (y, along_y))

    def rest_of_sum(hf):
        for j in range(2):
            for p in range(2):
                total = ring_last(hf, p, ring_out[j])
                own_part[j, hf, 4 * p : 4 * p + 4] = total
                part[j, hf, 4 * p : 4 * p + 4] = total.astype(BF16)

        def start(k):
            for j, (place, neighbour) in enumerate(others):
                to = (place + k) % N
                remote(part.at[j, hf, to], part_in.at[j, hf, place], S_P, p_recv.at[j, hf], neighbour(to)).start()

        loop(1, N, start)

    def finish(hf):
        for j, (place, _) in enumerate(others):
            take(part_in.at[j, hf, 0:7], p_recv.at[j, hf])
            total = own_part[j, hf, place]
            for k in range(1, N):
                total = total + part_in[j, hf, (place + k) % N].astype(F32)
            slab[16 * hf : 16 * hf + 16, 384 * j : 384 * (j + 1)] = total
        for p in range(4 * hf, 4 * hf + 4):
            fin_out[p] = slab[4 * p : 4 * p + 4]

            @pl.when(jnp.logical_and(y == c, p == y))
            def _():
                fin_in[c] = fin_out[p]

            @pl.when(jnp.logical_or(y != c, p != y))
            def _():
                remote(fin_out.at[p], fin_in.at[c], S_F, f_recv, dev(p, z, y)).start()

    gx, gh = Gather(x_buf, S_X, x_recv), Gather(h_buf, S_H, h_recv)
    x_own(0)
    gx.near(0)
    x_own(1)
    gx.far(0)
    gx.rest(0)
    own_w1.wait()
    take(w1.at[0:7], w_recv)
    pre_product(0)
    rings(0, 0, [ring_pre])
    gx.near(1)
    gx.far(1)
    rings(0, 1, [ring_pre])
    gx.rest(1)
    pre_product(1)
    rings(1, 0, [ring_pre])
    rings(0, 2, [ring_pre])
    rings(1, 1, [ring_pre])
    rings(0, 3, [ring_pre])
    rings(1, 2, [ring_pre])
    hidden(0)
    rings(1, 3, [ring_pre])
    hidden_on(0)
    hidden(1)
    own_w2.wait()
    h_own(0)
    hidden_on(1)
    gh.near(0)
    h_own(1)
    gh.far(0)
    gh.rest(0)
    out_product(0)
    rings(0, 0, ring_out)
    gh.near(1)
    rings(0, 1, ring_out)
    gh.far(1)
    gh.rest(1)
    out_product(1)
    rings(1, 0, ring_out)
    rings(0, 2, ring_out)
    rings(1, 1, ring_out)
    rings(0, 3, ring_out)
    rings(1, 2, ring_out)
    rest_of_sum(0)
    rings(1, 3, ring_out)
    finish(0)
    rest_of_sum(1)
    finish(1)

    drain(norm_out.at[0:7], S_Y)
    drain(w1.at[0:7], S_W)
    drain(x_buf.at[:, 0, 0:7], S_Z)
    for hf in range(2):
        drain(x_buf.at[hf, 0:7], S_X + hf)
        drain(h_buf.at[hf, 0:7], S_H + hf)
    for at in range(3):
        drain(ring_send.at[at, 0:7], S_R + at)
    drain(hid_out.at[:, 0:7], S_HC)
    drain(hid_in.at[:, 0:7], S_HY)
    drain(part.at[:, :, 0:7], S_P)

    @pl.when(y == c)
    def _():
        drain(fin_out.at[0:7], S_F)
        take(fin_in.at[0:7], f_recv)

    @pl.when(y != c)
    def _():
        drain(fin_out, S_F)
        take(fin_in, f_recv)

    for j in range(N):
        cols = slice(768 * j, 768 * (j + 1))
        out_ref[:, cols] = (tok_ref[:, cols].astype(F32) + fin_in[j]).astype(BF16)


def body(tokens, norm_gain, in_weight, out_weight):
    dma = pltpu.SemaphoreType.DMA
    return pl.pallas_call(
        kernel,
        out_shape=jax.ShapeDtypeStruct(tokens.shape, BF16),
        in_specs=[pl.BlockSpec(memory_space=pltpu.HBM)] * 4,
        out_specs=pl.BlockSpec(memory_space=pltpu.VMEM),
        scratch_shapes=[
            pltpu.VMEM((4, 6144), BF16),
            pltpu.VMEM((1, 6144), F32),
            pltpu.VMEM((N, 96, 384), BF16),
            pltpu.VMEM((384, 768), BF16),
            pltpu.VMEM((N, 4, 768), BF16),
            pltpu.VMEM((N, 4, 768), BF16),
            pltpu.VMEM((32, 768), F32),
            pltpu.VMEM((2, N, N, 16, 768), BF16),
            pltpu.VMEM((2, N, N, 16, 384), F32),
            pltpu.VMEM((2, N, 16, 384), BF16),
            pltpu.VMEM((2, N, 16, 384), BF16),
            pltpu.VMEM((2, N, N, 16, 384), BF16),
            pltpu.VMEM((2, N, N, 16, 768), F32),
            pltpu.VMEM((3, 8, 4, 64, 384), BF16),
            pltpu.VMEM((3, 8, 4, 64, 384), BF16),
            pltpu.VMEM((2, 2, N, 16, 384), BF16),
            pltpu.VMEM((2, 2, N, 16, 384), BF16),
            pltpu.VMEM((2, 2, N, 16, 384), F32),
            pltpu.VMEM((N, 4, 768), F32),
            pltpu.VMEM((N, 4, 768), F32),
            dma((4,)), dma((SENDS,)), dma, dma, dma((N,)), dma((2, 7)), dma((2, 7)), dma((2,)), dma((2,)),
            dma((3, 8, 4)), dma((2, 2)), dma,
        ],
        compiler_params=pltpu.CompilerParams(
            collective_id=0, has_side_effects=True, vmem_limit_bytes=62 * 1024 * 1024
        ),
        cost_estimate=pl.CostEstimate(flops=2_500_000_000, bytes_accessed=1_300_000, transcendentals=100_000),
    )(tokens, norm_gain.reshape(1, -1), in_weight, out_weight)


def solution(mesh):
    return jax.shard_map(
        body,
        mesh=mesh,
        in_specs=(P(("row", "col"), None), P(), P("row", "col"), P("row", "col")),
        out_specs=P(("row", "col"), None),
        check_vma=False,
    )
```

```python
import jax
import jax.numpy as jnp
from jax import lax
from jax.experimental import pallas as pl
from jax.experimental.pallas import tpu as pltpu
from jax.sharding import PartitionSpec as P

MESH = pl.DeviceIdType.MESH
N = 8
BF16 = jnp.bfloat16
F32 = jnp.float32


def gelu(v):
    return 0.5 * v * (1.0 + jnp.tanh(0.7978845608028654 * (v + 0.044715 * (v * v * v))))


def rows_of(block):
    return block.reshape(-1, block.shape[-1])


S_Y, S_W, S_Z, S_X, S_H, S_R, S_HC, S_HY, S_P, S_F, SENDS = 0, 1, 2, 3, 5, 7, 10, 11, 12, 13, 14


def kernel(
    tok_hbm, gain_hbm, inw_ref, outw_ref, out_ref,
    tok_ref, gain_ref, w1, w2, norm_out, norm_in, slab, x_buf, pre_own, own_out, sum_in, hid_in, h_buf, out_own,
    ring_send, ring_recv, part, part_in, own_part, fin_out, fin_in,
    w_sem, sent, y_recv, w_recv, z_recv, x_recv, h_recv, last_recv, own_recv, hy_recv, rs_recv, p_recv, f_recv,
):
    row, c = lax.axis_index("row"), lax.axis_index("col")
    y, z = row // N, row % N
    x, core = c // 2, c % 2

    def dev(y_at, z_at, c_at):
        return (y_at * N + z_at, c_at)

    def col_of(x_at, core_at):
        return ((x_at + 8) % 4) * 2 + core_at

    right, left, across, sibling = col_of(x + 1, core), col_of(x - 1, core), col_of(x + 2, core), col_of(x, 1 - core)

    def remote(src, dst, kind, recv, target):
        return pltpu.make_async_remote_copy(
            src_ref=src, dst_ref=dst, send_sem=sent.at[kind], recv_sem=recv, device_id=target, device_id_type=MESH
        )

    def take(ref, recv):
        remote(ref, ref, S_Y, recv, dev(y, z, sibling)).wait_recv()

    def drain(ref, kind):
        remote(ref, ref, kind, f_recv, dev(y, z, sibling)).wait_send()

    def loop(start, end, act):
        def step(k, _):
            act(k)
            return 0

        lax.fori_loop(start, end, step, 0)

    tok_in = pltpu.make_async_copy(tok_hbm, tok_ref, w_sem.at[2])
    gain_in = pltpu.make_async_copy(gain_hbm, gain_ref, w_sem.at[3])
    tok_in.start()
    gain_in.start()

    barrier = pltpu.get_barrier_semaphore()

    def greet(target):
        pl.semaphore_signal(barrier, inc=1, device_id=target, device_id_type=MESH)

    def greet_line(k):
        greet(dev((y + k) % N, z, c))
        greet(dev(y, (z + k) % N, c))
        greet(dev(y, z, (c + k) % N))

    def greet_plane(p):
        @pl.when(jnp.logical_or(y != c, p != c))
        def _():
            greet(dev(c, z, p))
            greet(dev(p, z, y))

        @pl.when(p != c)
        def _():
            greet(dev((y + 1) % N, z, p))
            greet(dev((y + N - 1) % N, z, p))

    loop(1, N, greet_line)
    loop(0, N, greet_plane)

    own_w1 = pltpu.make_async_copy(inw_ref.at[:, pl.ds(pl.multiple_of(z * 384, 384), 384)], w1.at[z], w_sem.at[0])
    own_w2 = pltpu.make_async_copy(outw_ref, w2, w_sem.at[1])
    own_w1.start()
    own_w2.start()

    tok_in.wait()
    gain_in.wait()
    values = tok_ref[...].astype(F32)
    center = jnp.mean(values, axis=1, keepdims=True)
    spread = jnp.mean(jnp.square(values - center), axis=1, keepdims=True)
    normed = ((values - center) / jnp.sqrt(spread + 1e-06) * gain_ref[...]).astype(BF16)
    for j in range(N):
        norm_out[j] = normed[:, 768 * j : 768 * (j + 1)]
    norm_in[pl.ds(y, 1)] = norm_out[pl.ds(y, 1)]

    @pl.when(y == c)
    def _():
        pl.semaphore_wait(barrier, 49)

    @pl.when(y != c)
    def _():
        pl.semaphore_wait(barrier, 51)

    def y_start(k):
        to = (y + k) % N
        remote(norm_out.at[to], norm_in.at[y], S_Y, y_recv, dev(to, z, c)).start()

    def w_start(k):
        to = (z + k) % N
        remote(
            inw_ref.at[:, pl.ds(pl.multiple_of(to * 384, 384), 384)], w1.at[z], S_W, w_recv, dev(y, to, c)
        ).start()

    loop(1, N, y_start)
    for k in (1, 7, 2, 6):
        w_start(k)
    take(norm_in.at[0:7], y_recv)
    for j in range(N):
        slab[4 * j : 4 * j + 4] = norm_in[j].astype(F32)
    for hf in range(2):
        x_buf[hf, c, z] = slab[16 * hf : 16 * hf + 16].astype(BF16)

    def z_copy(hf, at, shift):
        at, to = (z + at + N) % N, (z + shift + N) % N
        return remote(x_buf.at[hf, c, at], x_buf.at[hf, c, at], S_Z, z_recv.at[hf, at], dev(y, to, c))

    for hf in range(2):
        for shift in (2, -2, 1, -1):
            z_copy(hf, 0, shift).start()

    def z_take(hf, off):
        at = (z + off + N) % N
        take(x_buf.at[hf, c, at], z_recv.at[hf, at])

    def z_relay(hf):
        z_copy(hf, 2, -1).start()
        z_copy(hf, -2, 1).start()

        @pl.when(core == 0)
        def _():
            z_copy(hf, -2, 2).start()

        @pl.when(core == 1)
        def _():
            z_copy(hf, 2, -2).start()

    def x_send(hf, off):
        at = (z + off + N) % N
        block = x_buf.at[hf, c, at]
        for side, to in enumerate((right, left, across)):
            remote(block, block, S_X + hf, x_recv.at[hf, side], dev(y, z, to)).start()

    def x_own(hf):
        x_send(hf, 0)
        if hf == 0:
            for half in range(2):
                z_take(half, 2)
                z_take(half, -2)
                z_relay(half)
            for k in (3, 5, 4):
                w_start(k)
        for off in (2, -2):
            x_send(hf, off)
        for off in (1, -1, 3, -3, 4):
            z_take(hf, off)
            x_send(hf, off)
        remote(x_buf.at[hf, c], x_buf.at[hf, c], S_X + hf, x_recv.at[hf, 3], dev(y, z, sibling)).start()

    def h_own(hf):
        for off in (0, 1, -1, 2, -2, 3, -3, 4):
            at = (y + off + N) % N
            block = h_buf.at[hf, c, at]
            if off != 0:
                take(block, hy_recv.at[hf, at])
            for side, to in enumerate((right, left, across)):
                remote(block, block, S_H + hf, h_recv.at[hf, side], dev(y, z, to)).start()
        remote(h_buf.at[hf, c], h_buf.at[hf, c], S_H + hf, h_recv.at[hf, 3], dev(y, z, sibling)).start()

    class Gather:
        def __init__(self, buf, kind, recv):
            self.buf, self.kind, self.recv = buf, kind, recv

        def to_sibling(self, hf, side):
            block = self.buf.at[hf, (left, right, across)[side]]
            take(block, self.recv.at[hf, side])
            remote(block, block, self.kind + hf, self.recv.at[hf, 3], dev(y, z, sibling)).start()

        def near(self, hf):
            self.to_sibling(hf, 0)
            self.to_sibling(hf, 1)

        def far(self, hf):
            self.to_sibling(hf, 2)

        def rest(self, hf):
            take(self.buf.at[hf, 0:4], self.recv.at[hf, 3])

    def ring_copy(at, q, s, i, place, neighbour):
        way = 1 - 2 * (i % 2)
        return remote(
            ring_send.at[at, q, s], ring_recv.at[at, q, s], S_R + at, rs_recv.at[at, q, s], neighbour((place + way + N) % N)
        )

    def rings(hf, s, each):
        def step(i):
            odd = (i % 2 + i // 2) % 2
            q = hf * 4 + i

            def act():
                for at, place, neighbour, own in each:
                    to = (place + (1 - 2 * (i % 2)) * (4 - odd - s) + N) % N
                    mine = own(hf, to, i // 2)
                    if s > 0:
                        take(ring_recv.at[at, q, s - 1], rs_recv.at[at, q, s - 1])
                        mine = mine + ring_recv[at, q, s - 1].astype(F32)
                    ring_send[at, q, s] = mine.astype(BF16)
                    if at > 0 or s < 2:
                        ring_copy(at, q, s, i, place, neighbour).start()
                    elif s == 2:
                        pl.when(odd == 0)(lambda: ring_copy(at, q, s, i, place, neighbour).start())
                        pl.when(odd == 1)(lambda: scatter(hf, q, s, i))
                    else:
                        scatter(hf, q, s, i)

            if s < 3:
                act()
            else:
                pl.when(odd == 0)(act)

        loop(0, 4, step)

    def scatter(hf, q, s, i):
        to = (y + 1 - 2 * (i % 2) + N) % N
        for j in range(4):
            remote(
                ring_send.at[0, q, s, 16 * j : 16 * j + 16], sum_in.at[hf, i % 2, c], S_R, last_recv.at[hf],
                dev(to, z, i // 2 * 4 + j),
            ).start()

    def scatter_own(hf):
        own_out[hf] = pre_own[hf, y].astype(BF16)

        def start(k):
            to = (c + k) % N
            remote(own_out.at[hf, to], sum_in.at[hf, 2, c], S_HC, own_recv.at[hf], dev(y, z, to)).start()

        loop(1, N, start)
        sum_in[hf, 2, c] = own_out[hf, c]

    def ring_last(hf, p, ring):
        at, place, _, own = ring
        total = own(hf, place, p)
        for i in (2 * p, 2 * p + 1):
            q, s = hf * 4 + i, 3 - (p + i % 2) % 2
            take(ring_recv.at[at, q, s], rs_recv.at[at, q, s])
            total = total + ring_recv[at, q, s].astype(F32)
        return total.reshape(4, 16, 384)

    def along_y(to):
        return dev(to, z, c)

    def along_z(to):
        return dev(y, to, c)

    def pre_product(hf):
        def step(t):
            rows = rows_of(x_buf[hf, pl.ds(4 * t, 4)])
            sums = jnp.dot(rows, rows_of(w1[...]), preferred_element_type=F32)
            pre_own[hf, pl.ds(4 * t, 4)] = sums.reshape(4, N, 16, 384)

        loop(0, 2, step)

    def out_product(hf):
        def step(t):
            rows = rows_of(h_buf[hf, pl.ds(4 * t, 4)])
            sums = jnp.dot(rows, w2[...], preferred_element_type=F32)
            out_own[hf, pl.ds(4 * t, 4)] = sums.reshape(4, N, 16, 768)

        loop(0, 2, step)

    def pre_part(hf, to, p):
        return rows_of(pre_own[hf, to, pl.ds(4 * p, 4)])

    def out_part_a(hf, to, p):
        return rows_of(out_own[hf, pl.ds(4 * p, 4), to, :, 0:384])

    def out_part_b(hf, to, p):
        return rows_of(out_own[hf, to, pl.ds(4 * p, 4), :, 384:768])

    ring_pre = (0, y, along_y, pre_part)
    ring_out = ((1, y, along_y, out_part_a), (2, z, along_z, out_part_b))

    def pass_on(hf, of):
        @pl.when(of == y)
        def _():
            h_buf[hf, c, y] = hid_in[hf, of]

        @pl.when(of != y)
        def _():
            remote(hid_in.at[hf, of], h_buf.at[hf, c, y], S_HY, hy_recv.at[hf, y], dev(of, z, c)).start()

    def hidden(hf):
        take(sum_in.at[hf, 0:2], last_recv.at[hf])
        take(sum_in.at[hf, 2, 0:7], own_recv.at[hf])
        total = sum_in[hf, 0].astype(F32) + sum_in[hf, 1].astype(F32) + sum_in[hf, 2].astype(F32)
        hid_in[hf] = gelu(total).astype(BF16)
        loop(0, N, lambda of: pass_on(hf, of))

    others = ((z, along_z), (y, along_y))

    def rest_of_sum(hf):
        for j in range(2):
            for p in range(2):
                total = ring_last(hf, p, ring_out[j])
                own_part[j, hf, 4 * p : 4 * p + 4] = total
                part[j, hf, 4 * p : 4 * p + 4] = total.astype(BF16)

        def start(k):
            for j, (place, neighbour) in enumerate(others):
                to = (place + k) % N
                remote(part.at[j, hf, to], part_in.at[j, hf, place], S_P, p_recv.at[j, hf], neighbour(to)).start()

        loop(1, N, start)

    def finish(hf):
        for j, (place, _) in enumerate(others):
            take(part_in.at[j, hf, 0:7], p_recv.at[j, hf])
            total = own_part[j, hf, place]
            for k in range(1, N):
                total = total + part_in[j, hf, (place + k) % N].astype(F32)
            slab[16 * hf : 16 * hf + 16, 384 * j : 384 * (j + 1)] = total
        for p in range(4 * hf, 4 * hf + 4):
            fin_out[p] = slab[4 * p : 4 * p + 4].astype(BF16)

            @pl.when(jnp.logical_and(y == c, p == y))
            def _():
                fin_in[c] = fin_out[p]

            @pl.when(jnp.logical_or(y != c, p != y))
            def _():
                remote(fin_out.at[p], fin_in.at[c], S_F, f_recv, dev(p, z, y)).start()

    gx, gh = Gather(x_buf, S_X, x_recv), Gather(h_buf, S_H, h_recv)
    x_own(0)
    x_own(1)
    gx.near(0)
    gx.far(0)
    gx.rest(0)
    own_w1.wait()
    take(w1.at[0:7], w_recv)
    pre_product(0)
    rings(0, 0, [ring_pre])
    gx.near(1)
    gx.far(1)
    rings(0, 1, [ring_pre])
    scatter_own(0)
    gx.rest(1)
    pre_product(1)
    rings(1, 0, [ring_pre])
    rings(0, 2, [ring_pre])
    rings(1, 1, [ring_pre])
    scatter_own(1)
    rings(0, 3, [ring_pre])
    rings(1, 2, [ring_pre])
    hidden(0)
    rings(1, 3, [ring_pre])
    hidden(1)
    own_w2.wait()
    h_own(0)
    h_own(1)
    gh.near(0)
    gh.far(0)
    gh.rest(0)
    out_product(0)
    rings(0, 0, ring_out)
    gh.near(1)
    gh.far(1)
    rings(0, 1, ring_out)
    gh.rest(1)
    out_product(1)
    rings(1, 0, ring_out)
    rings(0, 2, ring_out)
    rings(1, 1, ring_out)
    rings(0, 3, ring_out)
    rings(1, 2, ring_out)
    rest_of_sum(0)
    rings(1, 3, ring_out)
    finish(0)
    rest_of_sum(1)
    finish(1)

    drain(norm_out.at[0:7], S_Y)
    drain(w1.at[0:7], S_W)
    drain(x_buf.at[:, 0, 0:7], S_Z)
    for hf in range(2):
        drain(x_buf.at[hf, 0:7], S_X + hf)
        drain(h_buf.at[hf, 0:7], S_H + hf)
    for at in range(3):
        drain(ring_send.at[at, 0:7], S_R + at)
    drain(own_out.at[:, 0:7], S_HC)
    drain(hid_in.at[:, 0:7], S_HY)
    drain(part.at[:, :, 0:7], S_P)

    @pl.when(y == c)
    def _():
        drain(fin_out.at[0:7], S_F)
        take(fin_in.at[0:7], f_recv)

    @pl.when(y != c)
    def _():
        drain(fin_out, S_F)
        take(fin_in, f_recv)

    for j in range(N):
        cols = slice(768 * j, 768 * (j + 1))
        out_ref[:, cols] = (tok_ref[:, cols].astype(F32) + fin_in[j].astype(F32)).astype(BF16)


def body(tokens, norm_gain, in_weight, out_weight):
    dma = pltpu.SemaphoreType.DMA
    return pl.pallas_call(
        kernel,
        out_shape=jax.ShapeDtypeStruct(tokens.shape, BF16),
        in_specs=[pl.BlockSpec(memory_space=pltpu.HBM)] * 4,
        out_specs=pl.BlockSpec(memory_space=pltpu.VMEM),
        scratch_shapes=[
            pltpu.VMEM((4, 6144), BF16),
            pltpu.VMEM((1, 6144), F32),
            pltpu.VMEM((N, 96, 384), BF16),
            pltpu.VMEM((384, 768), BF16),
            pltpu.VMEM((N, 4, 768), BF16),
            pltpu.VMEM((N, 4, 768), BF16),
            pltpu.VMEM((32, 768), F32),
            pltpu.VMEM((2, N, N, 16, 768), BF16),
            pltpu.VMEM((2, N, N, 16, 384), F32),
            pltpu.VMEM((2, N, 16, 384), BF16),
            pltpu.VMEM((2, 3, N, 16, 384), BF16),
            pltpu.VMEM((2, N, 16, 384), BF16),
            pltpu.VMEM((2, N, N, 16, 384), BF16),
            pltpu.VMEM((2, N, N, 16, 768), F32),
            pltpu.VMEM((3, 8, 4, 64, 384), BF16),
            pltpu.VMEM((3, 8, 4, 64, 384), BF16),
            pltpu.VMEM((2, 2, N, 16, 384), BF16),
            pltpu.VMEM((2, 2, N, 16, 384), BF16),
            pltpu.VMEM((2, 2, N, 16, 384), F32),
            pltpu.VMEM((N, 4, 768), BF16),
            pltpu.VMEM((N, 4, 768), BF16),
            dma((4,)), dma((SENDS,)), dma, dma, dma((2, N)), dma((2, 4)), dma((2, 4)), dma((2,)), dma((2,)), dma((2, N)),
            dma((3, 8, 4)), dma((2, 2)), dma,
        ],
        compiler_params=pltpu.CompilerParams(
            collective_id=0, has_side_effects=True, vmem_limit_bytes=62 * 1024 * 1024
        ),
        cost_estimate=pl.CostEstimate(flops=2_500_000_000, bytes_accessed=1_300_000, transcendentals=100_000),
    )(tokens, norm_gain.reshape(1, -1), in_weight, out_weight)


def solution(mesh):
    return jax.shard_map(
        body,
        mesh=mesh,
        in_specs=(P(("row", "col"), None), P(), P("row", "col"), P("row", "col")),
        out_specs=P(("row", "col"), None),
        check_vma=False,
    )
```

```python
import jax
import jax.numpy as jnp
from jax import lax
from jax.experimental import pallas as pl
from jax.experimental.pallas import tpu as pltpu
from jax.sharding import PartitionSpec as P

MESH = pl.DeviceIdType.MESH
N = 8
BF16 = jnp.bfloat16
F32 = jnp.float32


def gelu(v):
    return 0.5 * v * (1.0 + jnp.tanh(0.7978845608028654 * (v + 0.044715 * (v * v * v))))


def rows_of(block):
    return block.reshape(-1, block.shape[-1])


S_Y, S_W, S_Z, S_X, S_H, S_R, S_HC, S_HY, S_P, S_F, SENDS = 0, 1, 2, 3, 5, 7, 10, 11, 12, 13, 14


def kernel(
    tok_hbm, gain_hbm, inw_ref, outw_ref, out_ref,
    tok_ref, gain_ref, w1, w2, norm_out, norm_in, slab, x_buf, pre_own, own_out, sum_in, hid_in, h_buf, out_own,
    ring_send, ring_recv, part, part_in, own_part, fin_out, fin_in,
    w_sem, sent, y_recv, w_recv, z_recv, x_recv, h_recv, last_recv, own_recv, hy_recv, rs_recv, p_recv, f_recv,
):
    row, c = lax.axis_index("row"), lax.axis_index("col")
    y, z = row // N, row % N
    x, core = c // 2, c % 2

    def dev(y_at, z_at, c_at):
        return (y_at * N + z_at, c_at)

    def col_of(x_at, core_at):
        return ((x_at + 8) % 4) * 2 + core_at

    right, left, across, sibling = col_of(x + 1, core), col_of(x - 1, core), col_of(x + 2, core), col_of(x, 1 - core)

    def remote(src, dst, kind, recv, target):
        return pltpu.make_async_remote_copy(
            src_ref=src, dst_ref=dst, send_sem=sent.at[kind], recv_sem=recv, device_id=target, device_id_type=MESH
        )

    def take(ref, recv):
        remote(ref, ref, S_Y, recv, dev(y, z, sibling)).wait_recv()

    def drain(ref, kind):
        remote(ref, ref, kind, f_recv, dev(y, z, sibling)).wait_send()

    def loop(start, end, act):
        def step(k, _):
            act(k)
            return 0

        lax.fori_loop(start, end, step, 0)

    tok_in = pltpu.make_async_copy(tok_hbm, tok_ref, w_sem.at[2])
    gain_in = pltpu.make_async_copy(gain_hbm, gain_ref, w_sem.at[3])
    tok_in.start()
    gain_in.start()

    barrier = pltpu.get_barrier_semaphore()

    def greet(target):
        pl.semaphore_signal(barrier, inc=1, device_id=target, device_id_type=MESH)

    def greet_line(k):
        greet(dev((y + k) % N, z, c))
        greet(dev(y, (z + k) % N, c))
        greet(dev(y, z, (c + k) % N))

    def greet_plane(p):
        @pl.when(jnp.logical_or(y != c, p != c))
        def _():
            greet(dev(c, z, p))
            greet(dev(p, z, y))

        @pl.when(p != c)
        def _():
            greet(dev((y + 1) % N, z, p))
            greet(dev((y + N - 1) % N, z, p))

    loop(1, N, greet_line)
    loop(0, N, greet_plane)

    own_w1 = pltpu.make_async_copy(inw_ref.at[:, pl.ds(pl.multiple_of(z * 384, 384), 384)], w1.at[z], w_sem.at[0])
    own_w2 = [
        pltpu.make_async_copy(outw_ref.at[:, 384 * j : 384 * j + 384], w2.at[j], w_sem.at[(1, 4)[j]]) for j in range(2)
    ]
    own_w1.start()
    for copy in own_w2:
        copy.start()

    tok_in.wait()
    gain_in.wait()
    values = tok_ref[...].astype(F32)
    center = jnp.mean(values, axis=1, keepdims=True)
    spread = jnp.mean(jnp.square(values - center), axis=1, keepdims=True)
    normed = ((values - center) / jnp.sqrt(spread + 1e-06) * gain_ref[...]).astype(BF16)
    for j in range(N):
        norm_out[j] = normed[:, 768 * j : 768 * (j + 1)]
    norm_in[pl.ds(y, 1)] = norm_out[pl.ds(y, 1)]

    @pl.when(y == c)
    def _():
        pl.semaphore_wait(barrier, 49)

    @pl.when(y != c)
    def _():
        pl.semaphore_wait(barrier, 51)

    def y_start(k):
        to = (y + k) % N
        remote(norm_out.at[to], norm_in.at[y], S_Y, y_recv, dev(to, z, c)).start()

    def w_start(k):
        to = (z + k) % N
        remote(
            inw_ref.at[:, pl.ds(pl.multiple_of(to * 384, 384), 384)], w1.at[z], S_W, w_recv, dev(y, to, c)
        ).start()

    loop(1, N, y_start)
    for k in (1, 7, 2, 6):
        w_start(k)
    take(norm_in.at[0:7], y_recv)
    for j in range(N):
        slab[4 * j : 4 * j + 4] = norm_in[j].astype(F32)
    for hf in range(2):
        x_buf[hf, c, z] = slab[16 * hf : 16 * hf + 16].astype(BF16)

    def z_copy(hf, at, shift):
        at, to = (z + at + N) % N, (z + shift + N) % N
        return remote(x_buf.at[hf, c, at], x_buf.at[hf, c, at], S_Z, z_recv.at[hf, at], dev(y, to, c))

    for hf in range(2):
        for shift in (2, -2, 1, -1):
            z_copy(hf, 0, shift).start()

    def z_take(hf, off):
        at = (z + off + N) % N
        take(x_buf.at[hf, c, at], z_recv.at[hf, at])

    def z_relay(hf):
        z_copy(hf, 2, -1).start()
        z_copy(hf, -2, 1).start()

        @pl.when(core == 0)
        def _():
            z_copy(hf, -2, 2).start()

        @pl.when(core == 1)
        def _():
            z_copy(hf, 2, -2).start()

    def x_send(hf, off):
        at = (z + off + N) % N
        block = x_buf.at[hf, c, at]
        for side, to in enumerate((right, left, across)):
            remote(block, block, S_X + hf, x_recv.at[hf, side], dev(y, z, to)).start()

    def x_own(hf):
        x_send(hf, 0)
        if hf == 0:
            for half in range(2):
                z_take(half, 2)
                z_take(half, -2)
                z_relay(half)
            for k in (3, 5, 4):
                w_start(k)
        for off in (2, -2):
            x_send(hf, off)
        for off in (1, -1, 3, -3, 4):
            z_take(hf, off)
            x_send(hf, off)
        remote(x_buf.at[hf, c], x_buf.at[hf, c], S_X + hf, x_recv.at[hf, 3], dev(y, z, sibling)).start()

    def h_own(hf):
        for off in (0, 1, -1, 2, -2, 3, -3, 4):
            at = (y + off + N) % N
            block = h_buf.at[hf, c, at]
            if off != 0:
                take(block, hy_recv.at[hf, at])
            for side, to in enumerate((right, left, across)):
                remote(block, block, S_H + hf, h_recv.at[hf, side], dev(y, z, to)).start()
        remote(h_buf.at[hf, c], h_buf.at[hf, c], S_H + hf, h_recv.at[hf, 3], dev(y, z, sibling)).start()

    class Gather:
        def __init__(self, buf, kind, recv):
            self.buf, self.kind, self.recv = buf, kind, recv

        def to_sibling(self, hf, side):
            block = self.buf.at[hf, (left, right, across)[side]]
            take(block, self.recv.at[hf, side])
            remote(block, block, self.kind + hf, self.recv.at[hf, 3], dev(y, z, sibling)).start()

        def near(self, hf):
            self.to_sibling(hf, 0)
            self.to_sibling(hf, 1)

        def far(self, hf):
            self.to_sibling(hf, 2)

        def rest(self, hf):
            take(self.buf.at[hf, 0:4], self.recv.at[hf, 3])

    def ring_copy(at, q, s, i, place, neighbour):
        way = 1 - 2 * (i % 2)
        return remote(
            ring_send.at[at, q, s], ring_recv.at[at, q, s], S_R + at, rs_recv.at[at, q, s], neighbour((place + way + N) % N)
        )

    def rings(hf, s, each):
        def step(i):
            odd = (i % 2 + i // 2) % 2
            q = hf * 4 + i

            def act():
                for at, place, neighbour, own in each:
                    to = (place + (1 - 2 * (i % 2)) * (4 - odd - s) + N) % N
                    mine = own(hf, to, i // 2)
                    if s > 0:
                        take(ring_recv.at[at, q, s - 1], rs_recv.at[at, q, s - 1])
                        mine = mine + ring_recv[at, q, s - 1].astype(F32)
                    ring_send[at, q, s] = mine.astype(BF16)
                    if at > 0 or s < 2:
                        ring_copy(at, q, s, i, place, neighbour).start()
                    elif s == 2:
                        pl.when(odd == 0)(lambda: ring_copy(at, q, s, i, place, neighbour).start())
                        pl.when(odd == 1)(lambda: scatter(hf, q, s, i))
                    else:
                        scatter(hf, q, s, i)

            if s < 3:
                act()
            else:
                pl.when(odd == 0)(act)

        loop(0, 4, step)

    def scatter(hf, q, s, i):
        to = (y + 1 - 2 * (i % 2) + N) % N
        for j in range(4):
            remote(
                ring_send.at[0, q, s, 16 * j : 16 * j + 16], sum_in.at[hf, i % 2, c], S_R, last_recv.at[hf],
                dev(to, z, i // 2 * 4 + j),
            ).start()

    def scatter_own(hf):
        own_out[hf] = pre_own[hf, y].astype(BF16)

        def start(k):
            to = (c + k) % N
            remote(own_out.at[hf, to], sum_in.at[hf, 2, c], S_HC, own_recv.at[hf], dev(y, z, to)).start()

        loop(1, N, start)
        sum_in[hf, 2, c] = own_out[hf, c]

    def ring_last(hf, p, ring):
        at, place, _, own = ring
        total = own(hf, place, p)
        for i in (2 * p, 2 * p + 1):
            q, s = hf * 4 + i, 3 - (p + i % 2) % 2
            take(ring_recv.at[at, q, s], rs_recv.at[at, q, s])
            total = total + ring_recv[at, q, s].astype(F32)
        return total.reshape(4, 16, 384)

    def along_y(to):
        return dev(to, z, c)

    def along_z(to):
        return dev(y, to, c)

    FIRST, LATER = (4, 3, 5), (2, 6, 1, 7, 0)

    def pre_product(hf, offsets):
        for off in offsets:
            at = (y + off) % N
            sums = jnp.dot(rows_of(x_buf[hf, at]), rows_of(w1[...]), preferred_element_type=F32)
            pre_own[hf, at] = sums.reshape(N, 16, 384)

    def out_product(hf, offsets):
        for off in offsets:
            at = (y + off) % N
            sums = jnp.dot(rows_of(h_buf[hf, :, at]), w2[0], preferred_element_type=F32)
            out_own[0, hf, at] = sums.reshape(N, 16, 384)
            at = (z + off) % N
            sums = jnp.dot(rows_of(h_buf[hf, at]), w2[1], preferred_element_type=F32)
            out_own[1, hf, at] = sums.reshape(N, 16, 384)

    def pre_part(hf, to, p):
        return rows_of(pre_own[hf, to, pl.ds(4 * p, 4)])

    def out_part_a(hf, to, p):
        return rows_of(out_own[0, hf, to, pl.ds(4 * p, 4)])

    def out_part_b(hf, to, p):
        return rows_of(out_own[1, hf, to, pl.ds(4 * p, 4)])

    ring_pre = (0, y, along_y, pre_part)
    ring_out = ((1, y, along_y, out_part_a), (2, z, along_z, out_part_b))

    def pass_on(hf, of):
        @pl.when(of == y)
        def _():
            h_buf[hf, c, y] = hid_in[hf, of]

        @pl.when(of != y)
        def _():
            remote(hid_in.at[hf, of], h_buf.at[hf, c, y], S_HY, hy_recv.at[hf, y], dev(of, z, c)).start()

    def hidden(hf):
        take(sum_in.at[hf, 0:2], last_recv.at[hf])
        take(sum_in.at[hf, 2, 0:7], own_recv.at[hf])
        total = sum_in[hf, 0].astype(F32) + sum_in[hf, 1].astype(F32) + sum_in[hf, 2].astype(F32)
        hid_in[hf] = gelu(total).astype(BF16)
        loop(0, N, lambda of: pass_on(hf, of))

    others = ((z, along_z), (y, along_y))

    def rest_of_sum(hf):
        for j in range(2):
            for p in range(2):
                total = ring_last(hf, p, ring_out[j])
                own_part[j, hf, 4 * p : 4 * p + 4] = total
                part[j, hf, 4 * p : 4 * p + 4] = total.astype(BF16)

        def start(k):
            for j, (place, neighbour) in enumerate(others):
                to = (place + k) % N
                remote(part.at[j, hf, to], part_in.at[j, hf, place], S_P, p_recv.at[j, hf], neighbour(to)).start()

        loop(1, N, start)

    def finish(hf):
        for j, (place, _) in enumerate(others):
            take(part_in.at[j, hf, 0:7], p_recv.at[j, hf])
            total = own_part[j, hf, place]
            for k in range(1, N):
                total = total + part_in[j, hf, (place + k) % N].astype(F32)
            slab[16 * hf : 16 * hf + 16, 384 * j : 384 * (j + 1)] = total
        for p in range(4 * hf, 4 * hf + 4):
            fin_out[p] = slab[4 * p : 4 * p + 4].astype(BF16)

            @pl.when(jnp.logical_and(y == c, p == y))
            def _():
                fin_in[c] = fin_out[p]

            @pl.when(jnp.logical_or(y != c, p != y))
            def _():
                remote(fin_out.at[p], fin_in.at[c], S_F, f_recv, dev(p, z, y)).start()

    gx, gh = Gather(x_buf, S_X, x_recv), Gather(h_buf, S_H, h_recv)
    x_own(0)
    x_own(1)
    gx.near(0)
    gx.far(0)
    gx.rest(0)
    own_w1.wait()
    take(w1.at[0:7], w_recv)
    pre_product(0, FIRST)
    rings(0, 0, [ring_pre])
    pre_product(0, LATER)
    gx.near(1)
    gx.far(1)
    rings(0, 1, [ring_pre])
    scatter_own(0)
    gx.rest(1)
    pre_product(1, FIRST)
    rings(1, 0, [ring_pre])
    pre_product(1, LATER)
    rings(0, 2, [ring_pre])
    rings(1, 1, [ring_pre])
    scatter_own(1)
    rings(0, 3, [ring_pre])
    rings(1, 2, [ring_pre])
    hidden(0)
    rings(1, 3, [ring_pre])
    hidden(1)
    for copy in own_w2:
        copy.wait()
    h_own(0)
    h_own(1)
    gh.near(0)
    gh.far(0)
    gh.rest(0)
    out_product(0, FIRST)
    rings(0, 0, ring_out)
    out_product(0, LATER)
    gh.near(1)
    gh.far(1)
    rings(0, 1, ring_out)
    gh.rest(1)
    out_product(1, FIRST)
    rings(1, 0, ring_out)
    out_product(1, LATER)
    rings(0, 2, ring_out)
    rings(1, 1, ring_out)
    rings(0, 3, ring_out)
    rings(1, 2, ring_out)
    rest_of_sum(0)
    rings(1, 3, ring_out)
    finish(0)
    rest_of_sum(1)
    finish(1)

    drain(norm_out.at[0:7], S_Y)
    drain(w1.at[0:7], S_W)
    drain(x_buf.at[:, 0, 0:7], S_Z)
    for hf in range(2):
        drain(x_buf.at[hf, 0:7], S_X + hf)
        drain(h_buf.at[hf, 0:7], S_H + hf)
    for at in range(3):
        drain(ring_send.at[at, 0:7], S_R + at)
    drain(own_out.at[:, 0:7], S_HC)
    drain(hid_in.at[:, 0:7], S_HY)
    drain(part.at[:, :, 0:7], S_P)

    @pl.when(y == c)
    def _():
        drain(fin_out.at[0:7], S_F)
        take(fin_in.at[0:7], f_recv)

    @pl.when(y != c)
    def _():
        drain(fin_out, S_F)
        take(fin_in, f_recv)

    for j in range(N):
        cols = slice(768 * j, 768 * (j + 1))
        out_ref[:, cols] = (tok_ref[:, cols].astype(F32) + fin_in[j].astype(F32)).astype(BF16)


def body(tokens, norm_gain, in_weight, out_weight):
    dma = pltpu.SemaphoreType.DMA
    return pl.pallas_call(
        kernel,
        out_shape=jax.ShapeDtypeStruct(tokens.shape, BF16),
        in_specs=[pl.BlockSpec(memory_space=pltpu.HBM)] * 4,
        out_specs=pl.BlockSpec(memory_space=pltpu.VMEM),
        scratch_shapes=[
            pltpu.VMEM((4, 6144), BF16),
            pltpu.VMEM((1, 6144), F32),
            pltpu.VMEM((N, 96, 384), BF16),
            pltpu.VMEM((2, 384, 384), BF16),
            pltpu.VMEM((N, 4, 768), BF16),
            pltpu.VMEM((N, 4, 768), BF16),
            pltpu.VMEM((32, 768), F32),
            pltpu.VMEM((2, N, N, 16, 768), BF16),
            pltpu.VMEM((2, N, N, 16, 384), F32),
            pltpu.VMEM((2, N, 16, 384), BF16),
            pltpu.VMEM((2, 3, N, 16, 384), BF16),
            pltpu.VMEM((2, N, 16, 384), BF16),
            pltpu.VMEM((2, N, N, 16, 384), BF16),
            pltpu.VMEM((2, 2, N, N, 16, 384), F32),
            pltpu.VMEM((3, 8, 4, 64, 384), BF16),
            pltpu.VMEM((3, 8, 4, 64, 384), BF16),
            pltpu.VMEM((2, 2, N, 16, 384), BF16),
            pltpu.VMEM((2, 2, N, 16, 384), BF16),
            pltpu.VMEM((2, 2, N, 16, 384), F32),
            pltpu.VMEM((N, 4, 768), BF16),
            pltpu.VMEM((N, 4, 768), BF16),
            dma((5,)), dma((SENDS,)), dma, dma, dma((2, N)), dma((2, 4)), dma((2, 4)), dma((2,)), dma((2,)), dma((2, N)),
            dma((3, 8, 4)), dma((2, 2)), dma,
        ],
        compiler_params=pltpu.CompilerParams(
            collective_id=0, has_side_effects=True, vmem_limit_bytes=62 * 1024 * 1024
        ),
        cost_estimate=pl.CostEstimate(flops=2_500_000_000, bytes_accessed=1_300_000, transcendentals=100_000),
    )(tokens, norm_gain.reshape(1, -1), in_weight, out_weight)


def solution(mesh):
    return jax.shard_map(
        body,
        mesh=mesh,
        in_specs=(P(("row", "col"), None), P(), P("row", "col"), P("row", "col")),
        out_specs=P(("row", "col"), None),
        check_vma=False,
    )
```

```python
import jax
import jax.numpy as jnp
from jax import lax
from jax.experimental import pallas as pl
from jax.experimental.pallas import tpu as pltpu
from jax.sharding import PartitionSpec as P

MESH = pl.DeviceIdType.MESH
N = 8
BF16 = jnp.bfloat16
F32 = jnp.float32


def gelu(v):
    return 0.5 * v * (1.0 + jnp.tanh(0.7978845608028654 * (v + 0.044715 * (v * v * v))))


def rows_of(block):
    return block.reshape(-1, block.shape[-1])


S_Y, S_W, S_Z, S_X, S_H, S_R, S_HC, S_HY, S_P, S_F, SENDS = 0, 1, 2, 3, 5, 7, 10, 11, 12, 13, 14


def kernel(
    tok_hbm, gain_hbm, inw_ref, outw_ref, out_ref,
    tok_ref, gain_ref, w1, w2, norm_out, norm_in, slab, x_buf, pre_own, own_out, sum_in, hid_in, h_buf, out_own,
    ring_send, ring_recv, part, part_in, own_part, fin_out, fin_in,
    w_sem, sent, y_recv, w_recv, z_recv, x_recv, h_recv, last_recv, own_recv, hy_recv, rs_recv, p_recv, f_recv,
):
    row, c = lax.axis_index("row"), lax.axis_index("col")
    y, z = row // N, row % N
    x, core = c // 2, c % 2

    def dev(y_at, z_at, c_at):
        return (y_at * N + z_at, c_at)

    def col_of(x_at, core_at):
        return ((x_at + 8) % 4) * 2 + core_at

    right, left, across, sibling = col_of(x + 1, core), col_of(x - 1, core), col_of(x + 2, core), col_of(x, 1 - core)

    def remote(src, dst, kind, recv, target):
        return pltpu.make_async_remote_copy(
            src_ref=src, dst_ref=dst, send_sem=sent.at[kind], recv_sem=recv, device_id=target, device_id_type=MESH
        )

    def take(ref, recv):
        remote(ref, ref, S_Y, recv, dev(y, z, sibling)).wait_recv()

    def drain(ref, kind):
        remote(ref, ref, kind, f_recv, dev(y, z, sibling)).wait_send()

    def loop(start, end, act):
        def step(k, _):
            act(k)
            return 0

        lax.fori_loop(start, end, step, 0)

    tok_in = pltpu.make_async_copy(tok_hbm, tok_ref, w_sem.at[2])
    gain_in = pltpu.make_async_copy(gain_hbm, gain_ref, w_sem.at[3])
    tok_in.start()
    gain_in.start()

    barrier = pltpu.get_barrier_semaphore()

    def greet(target):
        pl.semaphore_signal(barrier, inc=1, device_id=target, device_id_type=MESH)

    def greet_line(k):
        greet(dev((y + k) % N, z, c))
        greet(dev(y, (z + k) % N, c))
        greet(dev(y, z, (c + k) % N))

    def greet_plane(p):
        @pl.when(jnp.logical_or(y != c, p != c))
        def _():
            greet(dev(c, z, p))
            greet(dev(p, z, y))

        @pl.when(p != c)
        def _():
            greet(dev((y + 1) % N, z, p))
            greet(dev((y + N - 1) % N, z, p))

    loop(1, N, greet_line)
    loop(0, N, greet_plane)

    own_w1 = pltpu.make_async_copy(inw_ref.at[:, pl.ds(pl.multiple_of(z * 384, 384), 384)], w1.at[z], w_sem.at[0])
    own_w2 = [
        pltpu.make_async_copy(outw_ref.at[:, 384 * j : 384 * j + 384], w2.at[j], w_sem.at[(1, 4)[j]]) for j in range(2)
    ]
    own_w1.start()
    for copy in own_w2:
        copy.start()

    tok_in.wait()
    gain_in.wait()
    values = tok_ref[...].astype(F32)
    center = jnp.mean(values, axis=1, keepdims=True)
    spread = jnp.mean(jnp.square(values - center), axis=1, keepdims=True)
    normed = ((values - center) / jnp.sqrt(spread + 1e-06) * gain_ref[...]).astype(BF16)
    for j in range(N):
        norm_out[j] = normed[:, 768 * j : 768 * (j + 1)]
    norm_in[pl.ds(y, 1)] = norm_out[pl.ds(y, 1)]

    @pl.when(y == c)
    def _():
        pl.semaphore_wait(barrier, 49)

    @pl.when(y != c)
    def _():
        pl.semaphore_wait(barrier, 51)

    def y_start(k):
        to = (y + k) % N
        remote(norm_out.at[to], norm_in.at[y], S_Y, y_recv, dev(to, z, c)).start()

    def w_start(k):
        to = (z + k) % N
        remote(
            inw_ref.at[:, pl.ds(pl.multiple_of(to * 384, 384), 384)], w1.at[z], S_W, w_recv, dev(y, to, c)
        ).start()

    loop(1, N, y_start)
    for k in (1, 7, 2, 6):
        w_start(k)
    take(norm_in.at[0:7], y_recv)
    for j in range(N):
        slab[4 * j : 4 * j + 4] = norm_in[j].astype(F32)
    for hf in range(2):
        x_buf[hf, c, z] = slab[16 * hf : 16 * hf + 16].astype(BF16)

    def z_copy(hf, at, shift):
        at, to = (z + at + N) % N, (z + shift + N) % N
        return remote(x_buf.at[hf, c, at], x_buf.at[hf, c, at], S_Z, z_recv.at[hf, at], dev(y, to, c))

    for hf in range(2):
        for shift in (2, -2, 1, -1):
            z_copy(hf, 0, shift).start()

    def z_take(hf, off):
        at = (z + off + N) % N
        take(x_buf.at[hf, c, at], z_recv.at[hf, at])

    def z_relay(hf):
        z_copy(hf, 2, -1).start()
        z_copy(hf, -2, 1).start()

        @pl.when(core == 0)
        def _():
            z_copy(hf, -2, 2).start()

        @pl.when(core == 1)
        def _():
            z_copy(hf, 2, -2).start()

    def x_send(hf, off):
        at = (z + off + N) % N
        block = x_buf.at[hf, c, at]
        for side, to in enumerate((right, left, across)):
            remote(block, block, S_X + hf, x_recv.at[hf, side], dev(y, z, to)).start()

    def x_own(hf):
        x_send(hf, 0)
        if hf == 0:
            z_take(0, 2)
            z_take(0, -2)
            z_relay(0)
        for off in (2, -2):
            x_send(hf, off)
        for off in (1, -1, 3, -3, 4):
            z_take(hf, off)
            x_send(hf, off)
            if hf == 0 and off == -1:
                z_take(1, 2)
                z_take(1, -2)
                z_relay(1)
                for k in (3, 5, 4):
                    w_start(k)
        remote(x_buf.at[hf, c], x_buf.at[hf, c], S_X + hf, x_recv.at[hf, 3], dev(y, z, sibling)).start()

    def h_own(hf, between=None):
        for off in (0, 1, -1, 2, -2, 3, -3, 4):
            if off == 3 and between is not None:
                between()
            at = (y + off + N) % N
            block = h_buf.at[hf, c, at]
            if off != 0:
                take(block, hy_recv.at[hf, at])
            for side, to in enumerate((right, left, across)):
                remote(block, block, S_H + hf, h_recv.at[hf, side], dev(y, z, to)).start()
        remote(h_buf.at[hf, c], h_buf.at[hf, c], S_H + hf, h_recv.at[hf, 3], dev(y, z, sibling)).start()

    class Gather:
        def __init__(self, buf, kind, recv):
            self.buf, self.kind, self.recv = buf, kind, recv

        def to_sibling(self, hf, side):
            block = self.buf.at[hf, (left, right, across)[side]]
            take(block, self.recv.at[hf, side])
            remote(block, block, self.kind + hf, self.recv.at[hf, 3], dev(y, z, sibling)).start()

        def near(self, hf):
            self.to_sibling(hf, 0)
            self.to_sibling(hf, 1)

        def far(self, hf):
            self.to_sibling(hf, 2)

        def rest(self, hf):
            take(self.buf.at[hf, 0:4], self.recv.at[hf, 3])

    def ring_copy(at, q, s, i, place, neighbour):
        way = 1 - 2 * (i % 2)
        return remote(
            ring_send.at[at, q, s], ring_recv.at[at, q, s], S_R + at, rs_recv.at[at, q, s], neighbour((place + way + N) % N)
        )

    def rings(hf, s, each):
        def step(i):
            odd = (i % 2 + i // 2) % 2
            q = hf * 4 + i

            def act():
                for at, place, neighbour, own in each:
                    to = (place + (1 - 2 * (i % 2)) * (4 - odd - s) + N) % N
                    mine = own(hf, to, i // 2)
                    if s > 0:
                        take(ring_recv.at[at, q, s - 1], rs_recv.at[at, q, s - 1])
                        mine = mine + ring_recv[at, q, s - 1].astype(F32)
                    ring_send[at, q, s] = mine.astype(BF16)
                    if at > 0 or s < 2:
                        ring_copy(at, q, s, i, place, neighbour).start()
                    elif s == 2:
                        pl.when(odd == 0)(lambda: ring_copy(at, q, s, i, place, neighbour).start())
                        pl.when(odd == 1)(lambda: scatter(hf, q, s, i))
                    else:
                        scatter(hf, q, s, i)

            if s < 3:
                act()
            else:
                pl.when(odd == 0)(act)

        loop(0, 4, step)

    def scatter(hf, q, s, i):
        to = (y + 1 - 2 * (i % 2) + N) % N
        for j in range(4):
            remote(
                ring_send.at[0, q, s, 16 * j : 16 * j + 16], sum_in.at[hf, i % 2, c], S_R, last_recv.at[hf],
                dev(to, z, i // 2 * 4 + j),
            ).start()

    def scatter_own(hf):
        own_out[hf] = pre_own[hf, y].astype(BF16)

        def start(k):
            to = (c + k) % N
            remote(own_out.at[hf, to], sum_in.at[hf, 2, c], S_HC, own_recv.at[hf], dev(y, z, to)).start()

        loop(1, N, start)
        sum_in[hf, 2, c] = own_out[hf, c]

    def ring_last(hf, p, ring):
        at, place, _, own = ring
        total = own(hf, place, p)
        for i in (2 * p, 2 * p + 1):
            q, s = hf * 4 + i, 3 - (p + i % 2) % 2
            take(ring_recv.at[at, q, s], rs_recv.at[at, q, s])
            total = total + ring_recv[at, q, s].astype(F32)
        return total.reshape(4, 16, 384)

    def along_y(to):
        return dev(to, z, c)

    def along_z(to):
        return dev(y, to, c)

    FIRST, LATER = (4, 3, 5), (2, 6, 1, 7, 0)

    def pre_product(hf, offsets):
        for off in offsets:
            at = (y + off) % N
            sums = jnp.dot(rows_of(x_buf[hf, at]), rows_of(w1[...]), preferred_element_type=F32)
            pre_own[hf, at] = sums.reshape(N, 16, 384)

    def out_product(hf, offsets):
        for off in offsets:
            at = (y + off) % N
            sums = jnp.dot(rows_of(h_buf[hf, :, at]), w2[0], preferred_element_type=F32)
            out_own[0, hf, at] = sums.reshape(N, 16, 384)
            at = (z + off) % N
            sums = jnp.dot(rows_of(h_buf[hf, at]), w2[1], preferred_element_type=F32)
            out_own[1, hf, at] = sums.reshape(N, 16, 384)

    def pre_part(hf, to, p):
        return rows_of(pre_own[hf, to, pl.ds(4 * p, 4)])

    def out_part_a(hf, to, p):
        return rows_of(out_own[0, hf, to, pl.ds(4 * p, 4)])

    def out_part_b(hf, to, p):
        return rows_of(out_own[1, hf, to, pl.ds(4 * p, 4)])

    ring_pre = (0, y, along_y, pre_part)
    ring_out = ((1, y, along_y, out_part_a), (2, z, along_z, out_part_b))

    def pass_on(hf, of):
        @pl.when(of == y)
        def _():
            h_buf[hf, c, y] = hid_in[hf, of]

        @pl.when(of != y)
        def _():
            remote(hid_in.at[hf, of], h_buf.at[hf, c, y], S_HY, hy_recv.at[hf, y], dev(of, z, c)).start()

    def hidden(hf):
        take(sum_in.at[hf, 0:2], last_recv.at[hf])
        take(sum_in.at[hf, 2, 0:7], own_recv.at[hf])
        total = sum_in[hf, 0].astype(F32) + sum_in[hf, 1].astype(F32) + sum_in[hf, 2].astype(F32)
        hid_in[hf] = gelu(total).astype(BF16)
        loop(0, N, lambda of: pass_on(hf, of))

    others = ((z, along_z), (y, along_y))

    def rest_of_sum(hf):
        for j in range(2):
            for p in range(2):
                total = ring_last(hf, p, ring_out[j])
                own_part[j, hf, 4 * p : 4 * p + 4] = total
                part[j, hf, 4 * p : 4 * p + 4] = total.astype(BF16)

        def start(k):
            for j, (place, neighbour) in enumerate(others):
                to = (place + k) % N
                remote(part.at[j, hf, to], part_in.at[j, hf, place], S_P, p_recv.at[j, hf], neighbour(to)).start()

        loop(1, N, start)

    def finish(hf):
        for j, (place, _) in enumerate(others):
            take(part_in.at[j, hf, 0:7], p_recv.at[j, hf])
            total = own_part[j, hf, place]
            for k in range(1, N):
                total = total + part_in[j, hf, (place + k) % N].astype(F32)
            slab[16 * hf : 16 * hf + 16, 384 * j : 384 * (j + 1)] = total
        for p in range(4 * hf, 4 * hf + 4):
            fin_out[p] = slab[4 * p : 4 * p + 4].astype(BF16)

            @pl.when(jnp.logical_and(y == c, p == y))
            def _():
                fin_in[c] = fin_out[p]

            @pl.when(jnp.logical_or(y != c, p != y))
            def _():
                remote(fin_out.at[p], fin_in.at[c], S_F, f_recv, dev(p, z, y)).start()

    gx, gh = Gather(x_buf, S_X, x_recv), Gather(h_buf, S_H, h_recv)
    x_own(0)
    x_own(1)
    gx.near(0)
    gx.far(0)
    gx.rest(0)
    own_w1.wait()
    take(w1.at[0:7], w_recv)
    pre_product(0, FIRST)
    rings(0, 0, [ring_pre])
    pre_product(0, LATER)
    gx.near(1)
    gx.far(1)
    rings(0, 1, [ring_pre])
    scatter_own(0)
    gx.rest(1)
    pre_product(1, FIRST)
    rings(1, 0, [ring_pre])
    pre_product(1, LATER)
    rings(0, 2, [ring_pre])
    rings(1, 1, [ring_pre])
    scatter_own(1)
    rings(0, 3, [ring_pre])
    rings(1, 2, [ring_pre])
    hidden(0)
    rings(1, 3, [ring_pre])
    for copy in own_w2:
        copy.wait()
    h_own(0)
    hidden(1)
    def pass_half_0():
        gh.near(0)
        gh.far(0)

    h_own(1, pass_half_0)
    gh.rest(0)
    out_product(0, FIRST)
    rings(0, 0, ring_out)
    out_product(0, LATER)
    gh.near(1)
    gh.far(1)
    rings(0, 1, ring_out)
    gh.rest(1)
    out_product(1, FIRST)
    rings(1, 0, ring_out)
    out_product(1, LATER)
    rings(0, 2, ring_out)
    rings(1, 1, ring_out)
    rings(0, 3, ring_out)
    rings(1, 2, ring_out)
    rest_of_sum(0)
    rings(1, 3, ring_out)
    rest_of_sum(1)
    finish(0)
    finish(1)

    drain(norm_out.at[0:7], S_Y)
    drain(w1.at[0:7], S_W)
    drain(x_buf.at[:, 0, 0:7], S_Z)
    for hf in range(2):
        drain(x_buf.at[hf, 0:7], S_X + hf)
        drain(h_buf.at[hf, 0:7], S_H + hf)
    for at in range(3):
        drain(ring_send.at[at, 0:7], S_R + at)
    drain(own_out.at[:, 0:7], S_HC)
    drain(hid_in.at[:, 0:7], S_HY)
    drain(part.at[:, :, 0:7], S_P)

    @pl.when(y == c)
    def _():
        drain(fin_out.at[0:7], S_F)
        take(fin_in.at[0:7], f_recv)

    @pl.when(y != c)
    def _():
        drain(fin_out, S_F)
        take(fin_in, f_recv)

    for j in range(N):
        cols = slice(768 * j, 768 * (j + 1))
        out_ref[:, cols] = (tok_ref[:, cols].astype(F32) + fin_in[j].astype(F32)).astype(BF16)


def body(tokens, norm_gain, in_weight, out_weight):
    dma = pltpu.SemaphoreType.DMA
    return pl.pallas_call(
        kernel,
        out_shape=jax.ShapeDtypeStruct(tokens.shape, BF16),
        in_specs=[pl.BlockSpec(memory_space=pltpu.HBM)] * 4,
        out_specs=pl.BlockSpec(memory_space=pltpu.VMEM),
        scratch_shapes=[
            pltpu.VMEM((4, 6144), BF16),
            pltpu.VMEM((1, 6144), F32),
            pltpu.VMEM((N, 96, 384), BF16),
            pltpu.VMEM((2, 384, 384), BF16),
            pltpu.VMEM((N, 4, 768), BF16),
            pltpu.VMEM((N, 4, 768), BF16),
            pltpu.VMEM((32, 768), F32),
            pltpu.VMEM((2, N, N, 16, 768), BF16),
            pltpu.VMEM((2, N, N, 16, 384), F32),
            pltpu.VMEM((2, N, 16, 384), BF16),
            pltpu.VMEM((2, 3, N, 16, 384), BF16),
            pltpu.VMEM((2, N, 16, 384), BF16),
            pltpu.VMEM((2, N, N, 16, 384), BF16),
            pltpu.VMEM((2, 2, N, N, 16, 384), F32),
            pltpu.VMEM((3, 8, 4, 64, 384), BF16),
            pltpu.VMEM((3, 8, 4, 64, 384), BF16),
            pltpu.VMEM((2, 2, N, 16, 384), BF16),
            pltpu.VMEM((2, 2, N, 16, 384), BF16),
            pltpu.VMEM((2, 2, N, 16, 384), F32),
            pltpu.VMEM((N, 4, 768), BF16),
            pltpu.VMEM((N, 4, 768), BF16),
            dma((5,)), dma((SENDS,)), dma, dma, dma((2, N)), dma((2, 4)), dma((2, 4)), dma((2,)), dma((2,)), dma((2, N)),
            dma((3, 8, 4)), dma((2, 2)), dma,
        ],
        compiler_params=pltpu.CompilerParams(
            collective_id=0, has_side_effects=True, vmem_limit_bytes=62 * 1024 * 1024
        ),
        cost_estimate=pl.CostEstimate(flops=2_500_000_000, bytes_accessed=1_300_000, transcendentals=100_000),
    )(tokens, norm_gain.reshape(1, -1), in_weight, out_weight)


def solution(mesh):
    return jax.shard_map(
        body,
        mesh=mesh,
        in_specs=(P(("row", "col"), None), P(), P("row", "col"), P("row", "col")),
        out_specs=P(("row", "col"), None),
        check_vma=False,
    )
```

```python
import jax
import jax.numpy as jnp
from jax import lax
from jax.experimental import pallas as pl
from jax.experimental.pallas import tpu as pltpu
from jax.sharding import PartitionSpec as P

MESH = pl.DeviceIdType.MESH
N = 8
BF16 = jnp.bfloat16
F32 = jnp.float32


def gelu(v):
    return 0.5 * v * (1.0 + jnp.tanh(0.7978845608028654 * (v + 0.044715 * (v * v * v))))


def rows_of(block):
    return block.reshape(-1, block.shape[-1])


S_Y, S_W, S_Z, S_X, S_H, S_R, S_HC, S_HY, S_P, S_F, SENDS = 0, 1, 2, 3, 5, 7, 10, 11, 12, 13, 14


def kernel(
    tok_hbm, gain_hbm, inw_ref, outw_ref, out_ref,
    tok_ref, gain_ref, w1, w2, norm_out, norm_in, slab, x_buf, pre_own, own_out, sum_in, hid_in, h_buf, out_own,
    ring_send, ring_recv, part, part_in, own_part, fin_out, fin_in,
    w_sem, sent, y_recv, w_recv, z_recv, x_recv, h_recv, last_recv, own_recv, hy_recv, rs_recv, p_recv, f_recv,
):
    row, c = lax.axis_index("row"), lax.axis_index("col")
    y, z = row // N, row % N
    x, core = c // 2, c % 2

    def dev(y_at, z_at, c_at):
        return (y_at * N + z_at, c_at)

    def col_of(x_at, core_at):
        return ((x_at + 8) % 4) * 2 + core_at

    right, left, across, sibling = col_of(x + 1, core), col_of(x - 1, core), col_of(x + 2, core), col_of(x, 1 - core)

    def remote(src, dst, kind, recv, target):
        return pltpu.make_async_remote_copy(
            src_ref=src, dst_ref=dst, send_sem=sent.at[kind], recv_sem=recv, device_id=target, device_id_type=MESH
        )

    def take(ref, recv):
        remote(ref, ref, S_Y, recv, dev(y, z, sibling)).wait_recv()

    def drain(ref, kind):
        remote(ref, ref, kind, f_recv, dev(y, z, sibling)).wait_send()

    def far_first(k):
        return 4 + (k // 2) * (2 * (k % 2) - 1)

    def loop(start, end, act):
        def step(k, _):
            act(k)
            return 0

        lax.fori_loop(start, end, step, 0)

    tok_in = pltpu.make_async_copy(tok_hbm, tok_ref, w_sem.at[2])
    gain_in = pltpu.make_async_copy(gain_hbm, gain_ref, w_sem.at[3])
    tok_in.start()
    gain_in.start()

    barrier = pltpu.get_barrier_semaphore()

    def greet(target):
        pl.semaphore_signal(barrier, inc=1, device_id=target, device_id_type=MESH)

    def greet_line(k):
        greet(dev((y + k) % N, z, c))
        greet(dev(y, (z + k) % N, c))
        greet(dev(y, z, (c + k) % N))

    def greet_plane(p):
        @pl.when(jnp.logical_or(y != c, p != c))
        def _():
            greet(dev(c, z, p))
            greet(dev(p, z, y))

        @pl.when(p != c)
        def _():
            greet(dev((y + 1) % N, z, p))
            greet(dev((y + N - 1) % N, z, p))

    loop(1, N, greet_line)
    loop(0, N, greet_plane)

    own_w1 = pltpu.make_async_copy(inw_ref.at[:, pl.ds(pl.multiple_of(z * 384, 384), 384)], w1.at[z], w_sem.at[0])
    own_w2 = [
        pltpu.make_async_copy(outw_ref.at[:, 384 * j : 384 * j + 384], w2.at[j], w_sem.at[(1, 4)[j]]) for j in range(2)
    ]
    own_w1.start()
    for copy in own_w2:
        copy.start()

    tok_in.wait()
    gain_in.wait()
    values = tok_ref[...].astype(F32)
    center = jnp.mean(values, axis=1, keepdims=True)
    spread = jnp.mean(jnp.square(values - center), axis=1, keepdims=True)
    normed = ((values - center) / jnp.sqrt(spread + 1e-06) * gain_ref[...]).astype(BF16)
    for j in range(N):
        norm_out[j] = normed[:, 768 * j : 768 * (j + 1)]
    norm_in[pl.ds(y, 1)] = norm_out[pl.ds(y, 1)]

    @pl.when(y == c)
    def _():
        pl.semaphore_wait(barrier, 49)

    @pl.when(y != c)
    def _():
        pl.semaphore_wait(barrier, 51)

    def y_start(k):
        to = (y + k) % N
        remote(norm_out.at[to], norm_in.at[y], S_Y, y_recv, dev(to, z, c)).start()

    def w_start(k):
        to = (z + k) % N
        remote(
            inw_ref.at[:, pl.ds(pl.multiple_of(to * 384, 384), 384)], w1.at[z], S_W, w_recv, dev(y, to, c)
        ).start()

    loop(1, N, lambda k: y_start(far_first(k)))
    for k in (1, 7, 2, 6):
        w_start(k)
    take(norm_in.at[0:7], y_recv)
    for j in range(N):
        slab[4 * j : 4 * j + 4] = norm_in[j].astype(F32)
    for hf in range(2):
        x_buf[hf, c, z] = slab[16 * hf : 16 * hf + 16].astype(BF16)

    def z_copy(hf, at, shift):
        at, to = (z + at + N) % N, (z + shift + N) % N
        return remote(x_buf.at[hf, c, at], x_buf.at[hf, c, at], S_Z, z_recv.at[hf, at], dev(y, to, c))

    for hf in range(2):
        for shift in (2, -2, 1, -1):
            z_copy(hf, 0, shift).start()

    def z_take(hf, off):
        at = (z + off + N) % N
        take(x_buf.at[hf, c, at], z_recv.at[hf, at])

    def z_relay(hf):
        z_copy(hf, 2, -1).start()
        z_copy(hf, -2, 1).start()

        @pl.when(core == 0)
        def _():
            z_copy(hf, -2, 2).start()

        @pl.when(core == 1)
        def _():
            z_copy(hf, 2, -2).start()

    def x_send(hf, off):
        at = (z + off + N) % N
        block = x_buf.at[hf, c, at]
        for side, to in ((2, across), (0, right), (1, left)):
            remote(block, block, S_X + hf, x_recv.at[hf, side], dev(y, z, to)).start()

    def x_own(hf):
        x_send(hf, 0)
        if hf == 0:
            z_take(0, 2)
            z_take(0, -2)
            z_relay(0)
        for off in (2, -2):
            x_send(hf, off)
        for off in (1, -1, 3, -3, 4):
            z_take(hf, off)
            x_send(hf, off)
            if hf == 0 and off == -1:
                z_take(1, 2)
                z_take(1, -2)
                z_relay(1)
                for k in (3, 5, 4):
                    w_start(k)
        remote(x_buf.at[hf, c], x_buf.at[hf, c], S_X + hf, x_recv.at[hf, 3], dev(y, z, sibling)).start()

    def h_own(hf, between=None):
        for off in (0, 1, -1, 2, -2, 3, -3, 4):
            if off == 3 and between is not None:
                between()
            at = (y + off + N) % N
            block = h_buf.at[hf, c, at]
            if off != 0:
                take(block, hy_recv.at[hf, at])
            for side, to in ((2, across), (0, right), (1, left)):
                remote(block, block, S_H + hf, h_recv.at[hf, side], dev(y, z, to)).start()
        remote(h_buf.at[hf, c], h_buf.at[hf, c], S_H + hf, h_recv.at[hf, 3], dev(y, z, sibling)).start()

    class Gather:
        def __init__(self, buf, kind, recv):
            self.buf, self.kind, self.recv = buf, kind, recv

        def to_sibling(self, hf, side):
            block = self.buf.at[hf, (left, right, across)[side]]
            take(block, self.recv.at[hf, side])
            remote(block, block, self.kind + hf, self.recv.at[hf, 3], dev(y, z, sibling)).start()

        def near(self, hf):
            self.to_sibling(hf, 0)
            self.to_sibling(hf, 1)

        def far(self, hf):
            self.to_sibling(hf, 2)

        def rest(self, hf):
            take(self.buf.at[hf, 0:4], self.recv.at[hf, 3])

    def ring_copy(at, q, s, i, place, neighbour):
        way = 1 - 2 * (i % 2)
        return remote(
            ring_send.at[at, q, s], ring_recv.at[at, q, s], S_R + at, rs_recv.at[at, q, s], neighbour((place + way + N) % N)
        )

    def rings(hf, s, each):
        def step(i):
            odd = (i % 2 + i // 2) % 2
            q = hf * 4 + i

            def act():
                for at, place, neighbour, own in each:
                    to = (place + (1 - 2 * (i % 2)) * (4 - odd - s) + N) % N
                    mine = own(hf, to, i // 2)
                    if s > 0:
                        take(ring_recv.at[at, q, s - 1], rs_recv.at[at, q, s - 1])
                        mine = mine + ring_recv[at, q, s - 1].astype(F32)
                    ring_send[at, q, s] = mine.astype(BF16)
                    if at > 0 or s < 2:
                        ring_copy(at, q, s, i, place, neighbour).start()
                    elif s == 2:
                        pl.when(odd == 0)(lambda: ring_copy(at, q, s, i, place, neighbour).start())
                        pl.when(odd == 1)(lambda: scatter(hf, q, s, i))
                    else:
                        scatter(hf, q, s, i)

            if s < 3:
                act()
            else:
                pl.when(odd == 0)(act)

        loop(0, 4, step)

    def scatter(hf, q, s, i):
        to = (y + 1 - 2 * (i % 2) + N) % N
        for j in range(4):
            remote(
                ring_send.at[0, q, s, 16 * j : 16 * j + 16], sum_in.at[hf, i % 2, c], S_R, last_recv.at[hf],
                dev(to, z, i // 2 * 4 + j),
            ).start()

    def scatter_own(hf):
        own_out[hf] = pre_own[hf, y].astype(BF16)

        def start(k):
            to = (c + k) % N
            remote(own_out.at[hf, to], sum_in.at[hf, 2, c], S_HC, own_recv.at[hf], dev(y, z, to)).start()

        loop(1, N, start)
        sum_in[hf, 2, c] = own_out[hf, c]

    def ring_last(hf, p, ring):
        at, place, _, own = ring
        total = own(hf, place, p)
        for i in (2 * p, 2 * p + 1):
            q, s = hf * 4 + i, 3 - (p + i % 2) % 2
            take(ring_recv.at[at, q, s], rs_recv.at[at, q, s])
            total = total + ring_recv[at, q, s].astype(F32)
        return total.reshape(4, 16, 384)

    def along_y(to):
        return dev(to, z, c)

    def along_z(to):
        return dev(y, to, c)

    FIRST, LATER = (4, 3, 5), (2, 6, 1, 7, 0)

    def pre_product(hf, offsets):
        for off in offsets:
            at = (y + off) % N
            sums = jnp.dot(rows_of(x_buf[hf, at]), rows_of(w1[...]), preferred_element_type=F32)
            pre_own[hf, at] = sums.reshape(N, 16, 384)

    def out_product(hf, offsets):
        for off in offsets:
            at = (y + off) % N
            sums = jnp.dot(rows_of(h_buf[hf, :, at]), w2[0], preferred_element_type=F32)
            out_own[0, hf, at] = sums.reshape(N, 16, 384)
            at = (z + off) % N
            sums = jnp.dot(rows_of(h_buf[hf, at]), w2[1], preferred_element_type=F32)
            out_own[1, hf, at] = sums.reshape(N, 16, 384)

    def pre_part(hf, to, p):
        return rows_of(pre_own[hf, to, pl.ds(4 * p, 4)])

    def out_part_a(hf, to, p):
        return rows_of(out_own[0, hf, to, pl.ds(4 * p, 4)])

    def out_part_b(hf, to, p):
        return rows_of(out_own[1, hf, to, pl.ds(4 * p, 4)])

    ring_pre = (0, y, along_y, pre_part)
    ring_out = ((1, y, along_y, out_part_a), (2, z, along_z, out_part_b))

    def pass_on(hf, of):
        remote(hid_in.at[hf, of], h_buf.at[hf, c, y], S_HY, hy_recv.at[hf, y], dev(of, z, c)).start()

    def hidden(hf):
        take(sum_in.at[hf, 0:2], last_recv.at[hf])
        take(sum_in.at[hf, 2, 0:7], own_recv.at[hf])
        total = sum_in[hf, 0].astype(F32) + sum_in[hf, 1].astype(F32) + sum_in[hf, 2].astype(F32)
        hid_in[hf] = gelu(total).astype(BF16)
        loop(1, N, lambda k: pass_on(hf, (y + far_first(k)) % N))
        h_buf[hf, c, y] = hid_in[hf, y]

    others = ((z, along_z), (y, along_y))

    def rest_of_sum(hf):
        def send(j, to):
            place, neighbour = others[j]

            @pl.when(to != place)
            def _():
                remote(part.at[j, hf, to], part_in.at[j, hf, place], S_P, p_recv.at[j, hf], neighbour(to)).start()

        for p in range(2):
            for j in range(2):
                total = ring_last(hf, p, ring_out[j])
                own_part[j, hf, 4 * p : 4 * p + 4] = total
                part[j, hf, 4 * p : 4 * p + 4] = total.astype(BF16)
                for to in range(4 * p, 4 * p + 4):
                    send(j, to)

    def finish(hf):
        for j, (place, _) in enumerate(others):
            take(part_in.at[j, hf, 0:7], p_recv.at[j, hf])
            total = own_part[j, hf, place]
            for k in range(1, N):
                total = total + part_in[j, hf, (place + k) % N].astype(F32)
            slab[16 * hf : 16 * hf + 16, 384 * j : 384 * (j + 1)] = total
        for p in range(4 * hf, 4 * hf + 4):
            fin_out[p] = slab[4 * p : 4 * p + 4].astype(BF16)

            @pl.when(jnp.logical_and(y == c, p == y))
            def _():
                fin_in[c] = fin_out[p]

            @pl.when(jnp.logical_or(y != c, p != y))
            def _():
                remote(fin_out.at[p], fin_in.at[c], S_F, f_recv, dev(p, z, y)).start()

    gx, gh = Gather(x_buf, S_X, x_recv), Gather(h_buf, S_H, h_recv)
    x_own(0)
    x_own(1)
    gx.near(0)
    gx.far(0)
    gx.rest(0)
    own_w1.wait()
    take(w1.at[0:7], w_recv)
    pre_product(0, FIRST)
    rings(0, 0, [ring_pre])
    pre_product(0, LATER)
    gx.near(1)
    gx.far(1)
    rings(0, 1, [ring_pre])
    scatter_own(0)
    gx.rest(1)
    pre_product(1, FIRST)
    rings(1, 0, [ring_pre])
    pre_product(1, LATER)
    rings(0, 2, [ring_pre])
    rings(1, 1, [ring_pre])
    scatter_own(1)
    rings(0, 3, [ring_pre])
    rings(1, 2, [ring_pre])
    hidden(0)
    rings(1, 3, [ring_pre])
    for copy in own_w2:
        copy.wait()
    h_own(0)
    hidden(1)
    def pass_half_0():
        gh.near(0)
        gh.far(0)

    h_own(1, pass_half_0)
    gh.rest(0)
    out_product(0, FIRST)
    rings(0, 0, ring_out)
    out_product(0, LATER)
    gh.near(1)
    gh.far(1)
    rings(0, 1, ring_out)
    gh.rest(1)
    out_product(1, FIRST)
    rings(1, 0, ring_out)
    out_product(1, LATER)
    rings(0, 2, ring_out)
    rings(1, 1, ring_out)
    rings(0, 3, ring_out)
    rings(1, 2, ring_out)
    rest_of_sum(0)
    rings(1, 3, ring_out)
    rest_of_sum(1)
    finish(0)
    finish(1)

    drain(norm_out.at[0:7], S_Y)
    drain(w1.at[0:7], S_W)
    drain(x_buf.at[:, 0, 0:7], S_Z)
    for hf in range(2):
        drain(x_buf.at[hf, 0:7], S_X + hf)
        drain(h_buf.at[hf, 0:7], S_H + hf)
    for at in range(3):
        drain(ring_send.at[at, 0:7], S_R + at)
    drain(own_out.at[:, 0:7], S_HC)
    drain(hid_in.at[:, 0:7], S_HY)
    drain(part.at[:, :, 0:7], S_P)

    @pl.when(y == c)
    def _():
        drain(fin_out.at[0:7], S_F)
        take(fin_in.at[0:7], f_recv)

    @pl.when(y != c)
    def _():
        drain(fin_out, S_F)
        take(fin_in, f_recv)

    for j in range(N):
        cols = slice(768 * j, 768 * (j + 1))
        out_ref[:, cols] = (tok_ref[:, cols].astype(F32) + fin_in[j].astype(F32)).astype(BF16)


def body(tokens, norm_gain, in_weight, out_weight):
    dma = pltpu.SemaphoreType.DMA
    return pl.pallas_call(
        kernel,
        out_shape=jax.ShapeDtypeStruct(tokens.shape, BF16),
        in_specs=[pl.BlockSpec(memory_space=pltpu.HBM)] * 4,
        out_specs=pl.BlockSpec(memory_space=pltpu.VMEM),
        scratch_shapes=[
            pltpu.VMEM((4, 6144), BF16),
            pltpu.VMEM((1, 6144), F32),
            pltpu.VMEM((N, 96, 384), BF16),
            pltpu.VMEM((2, 384, 384), BF16),
            pltpu.VMEM((N, 4, 768), BF16),
            pltpu.VMEM((N, 4, 768), BF16),
            pltpu.VMEM((32, 768), F32),
            pltpu.VMEM((2, N, N, 16, 768), BF16),
            pltpu.VMEM((2, N, N, 16, 384), F32),
            pltpu.VMEM((2, N, 16, 384), BF16),
            pltpu.VMEM((2, 3, N, 16, 384), BF16),
            pltpu.VMEM((2, N, 16, 384), BF16),
            pltpu.VMEM((2, N, N, 16, 384), BF16),
            pltpu.VMEM((2, 2, N, N, 16, 384), F32),
            pltpu.VMEM((3, 8, 4, 64, 384), BF16),
            pltpu.VMEM((3, 8, 4, 64, 384), BF16),
            pltpu.VMEM((2, 2, N, 16, 384), BF16),
            pltpu.VMEM((2, 2, N, 16, 384), BF16),
            pltpu.VMEM((2, 2, N, 16, 384), F32),
            pltpu.VMEM((N, 4, 768), BF16),
            pltpu.VMEM((N, 4, 768), BF16),
            dma((5,)), dma((SENDS,)), dma, dma, dma((2, N)), dma((2, 4)), dma((2, 4)), dma((2,)), dma((2,)), dma((2, N)),
            dma((3, 8, 4)), dma((2, 2)), dma,
        ],
        compiler_params=pltpu.CompilerParams(
            collective_id=0, has_side_effects=True, vmem_limit_bytes=62 * 1024 * 1024
        ),
        cost_estimate=pl.CostEstimate(flops=2_500_000_000, bytes_accessed=1_300_000, transcendentals=100_000),
    )(tokens, norm_gain.reshape(1, -1), in_weight, out_weight)


def solution(mesh):
    return jax.shard_map(
        body,
        mesh=mesh,
        in_specs=(P(("row", "col"), None), P(), P("row", "col"), P("row", "col")),
        out_specs=P(("row", "col"), None),
        check_vma=False,
    )
```

```python
import jax
import jax.numpy as jnp
from jax import lax
from jax.experimental import pallas as pl
from jax.experimental.pallas import tpu as pltpu
from jax.sharding import PartitionSpec as P

MESH = pl.DeviceIdType.MESH
N = 8
BF16 = jnp.bfloat16
F32 = jnp.float32


def gelu(v):
    return 0.5 * v * (1.0 + jnp.tanh(0.7978845608028654 * (v + 0.044715 * (v * v * v))))


def rows_of(block):
    return block.reshape(-1, block.shape[-1])


S_Y, S_W, S_Z, S_X, S_H, S_R, S_HC, S_HY, S_P, S_F, SENDS = 0, 1, 2, 3, 5, 7, 10, 11, 12, 13, 14


def kernel(
    tok_hbm, gain_hbm, inw_ref, outw_ref, out_ref,
    tok_ref, gain_ref, w1, w2, norm_out, norm_in, slab, x_buf, pre_own, own_out, sum_in, hid_in, h_buf, out_own,
    ring_send, ring_recv, part, part_in, own_part, fin_out, fin_in,
    w_sem, sent, y_recv, w_recv, z_recv, x_recv, h_recv, last_recv, own_recv, hy_recv, rs_recv, p_recv, f_recv,
):
    row, c = lax.axis_index("row"), lax.axis_index("col")
    y, z = row // N, row % N
    x, core = c // 2, c % 2

    def dev(y_at, z_at, c_at):
        return (y_at * N + z_at, c_at)

    def col_of(x_at, core_at):
        return ((x_at + 8) % 4) * 2 + core_at

    right, left, across, sibling = col_of(x + 1, core), col_of(x - 1, core), col_of(x + 2, core), col_of(x, 1 - core)

    def remote(src, dst, kind, recv, target):
        return pltpu.make_async_remote_copy(
            src_ref=src, dst_ref=dst, send_sem=sent.at[kind], recv_sem=recv, device_id=target, device_id_type=MESH
        )

    def take(ref, recv):
        remote(ref, ref, S_Y, recv, dev(y, z, sibling)).wait_recv()

    def drain(ref, kind):
        remote(ref, ref, kind, f_recv, dev(y, z, sibling)).wait_send()

    def far_first(k):
        return 4 + (k // 2) * (2 * (k % 2) - 1)

    def loop(start, end, act):
        def step(k, _):
            act(k)
            return 0

        lax.fori_loop(start, end, step, 0)

    tok_in = pltpu.make_async_copy(tok_hbm, tok_ref, w_sem.at[2])
    gain_in = pltpu.make_async_copy(gain_hbm, gain_ref, w_sem.at[3])
    tok_in.start()
    gain_in.start()

    barrier = pltpu.get_barrier_semaphore()

    def greet(target):
        pl.semaphore_signal(barrier, inc=1, device_id=target, device_id_type=MESH)

    def greet_line(k):
        greet(dev((y + k) % N, z, c))
        greet(dev(y, (z + k) % N, c))
        greet(dev(y, z, (c + k) % N))

    loop(1, N, greet_line)

    own_w1 = pltpu.make_async_copy(inw_ref.at[:, pl.ds(pl.multiple_of(z * 384, 384), 384)], w1.at[z], w_sem.at[0])
    own_w2 = [
        pltpu.make_async_copy(outw_ref.at[:, 384 * j : 384 * j + 384], w2.at[j], w_sem.at[(1, 4)[j]]) for j in range(2)
    ]
    own_w1.start()
    for copy in own_w2:
        copy.start()

    tok_in.wait()
    gain_in.wait()
    values = tok_ref[...].astype(F32)
    center = jnp.mean(values, axis=1, keepdims=True)
    spread = jnp.mean(jnp.square(values - center), axis=1, keepdims=True)
    normed = ((values - center) / jnp.sqrt(spread + 1e-06) * gain_ref[...]).astype(BF16)
    for j in range(N):
        norm_out[j] = normed[:, 768 * j : 768 * (j + 1)]
    norm_in[pl.ds(y, 1)] = norm_out[pl.ds(y, 1)]

    pl.semaphore_wait(barrier, 21)

    def y_start(k):
        to = (y + k) % N
        remote(norm_out.at[to], norm_in.at[y], S_Y, y_recv, dev(to, z, c)).start()

    def w_start(k):
        to = (z + k) % N
        remote(
            inw_ref.at[:, pl.ds(pl.multiple_of(to * 384, 384), 384)], w1.at[z], S_W, w_recv, dev(y, to, c)
        ).start()

    loop(1, N, lambda k: y_start(far_first(k)))
    for k in (1, 7, 2, 6):
        w_start(k)
    take(norm_in.at[0:7], y_recv)
    for j in range(N):
        slab[4 * j : 4 * j + 4] = norm_in[j].astype(F32)
    for hf in range(2):
        x_buf[hf, c, z] = slab[16 * hf : 16 * hf + 16].astype(BF16)

    def z_copy(hf, at, shift):
        at, to = (z + at + N) % N, (z + shift + N) % N
        return remote(x_buf.at[hf, c, at], x_buf.at[hf, c, at], S_Z, z_recv.at[hf, at], dev(y, to, c))

    for hf in range(2):
        for shift in (2, -2, 1, -1):
            z_copy(hf, 0, shift).start()

    def z_take(hf, off):
        at = (z + off + N) % N
        take(x_buf.at[hf, c, at], z_recv.at[hf, at])

    def z_relay(hf):
        z_copy(hf, 2, -1).start()
        z_copy(hf, -2, 1).start()

        @pl.when(core == 0)
        def _():
            z_copy(hf, -2, 2).start()

        @pl.when(core == 1)
        def _():
            z_copy(hf, 2, -2).start()

    def x_send(hf, off):
        at = (z + off + N) % N
        block = x_buf.at[hf, c, at]
        for side, to in ((2, across), (0, right), (1, left)):
            remote(block, block, S_X + hf, x_recv.at[hf, side], dev(y, z, to)).start()

    def x_own(hf):
        x_send(hf, 0)
        if hf == 0:
            z_take(0, 2)
            z_take(0, -2)
            z_relay(0)
        for off in (2, -2):
            x_send(hf, off)
        for off in (1, -1, 3, -3, 4):
            z_take(hf, off)
            x_send(hf, off)
            if hf == 0 and off == -1:
                z_take(1, 2)
                z_take(1, -2)
                z_relay(1)
                for k in (3, 5, 4):
                    w_start(k)
        remote(x_buf.at[hf, c], x_buf.at[hf, c], S_X + hf, x_recv.at[hf, 3], dev(y, z, sibling)).start()

    def h_own(hf, between=None):
        for off in (0, 1, -1, 2, -2, 3, -3, 4):
            if off == 3 and between is not None:
                between()
            at = (y + off + N) % N
            block = h_buf.at[hf, c, at]
            if off != 0:
                take(block, hy_recv.at[hf, at])
            for side, to in ((2, across), (0, right), (1, left)):
                remote(block, block, S_H + hf, h_recv.at[hf, side], dev(y, z, to)).start()
        remote(h_buf.at[hf, c], h_buf.at[hf, c], S_H + hf, h_recv.at[hf, 3], dev(y, z, sibling)).start()

    class Gather:
        def __init__(self, buf, kind, recv):
            self.buf, self.kind, self.recv = buf, kind, recv

        def to_sibling(self, hf, side):
            block = self.buf.at[hf, (left, right, across)[side]]
            take(block, self.recv.at[hf, side])
            remote(block, block, self.kind + hf, self.recv.at[hf, 3], dev(y, z, sibling)).start()

        def near(self, hf):
            self.to_sibling(hf, 0)
            self.to_sibling(hf, 1)

        def far(self, hf):
            self.to_sibling(hf, 2)

        def rest(self, hf):
            take(self.buf.at[hf, 0:4], self.recv.at[hf, 3])

    def ring_copy(at, q, s, i, place, neighbour):
        way = 1 - 2 * (i % 2)
        return remote(
            ring_send.at[at, q, s], ring_recv.at[at, q, s], S_R + at, rs_recv.at[at, q, s], neighbour((place + way + N) % N)
        )

    def rings(hf, s, each):
        def step(i):
            odd = (i % 2 + i // 2) % 2
            q = hf * 4 + i

            def act():
                for at, place, neighbour, own in each:
                    to = (place + (1 - 2 * (i % 2)) * (4 - odd - s) + N) % N
                    mine = own(hf, to, i // 2)
                    if s > 0:
                        take(ring_recv.at[at, q, s - 1], rs_recv.at[at, q, s - 1])
                        mine = mine + ring_recv[at, q, s - 1].astype(F32)
                    ring_send[at, q, s] = mine.astype(BF16)
                    if at > 0 or s < 2:
                        ring_copy(at, q, s, i, place, neighbour).start()
                    elif s == 2:
                        pl.when(odd == 0)(lambda: ring_copy(at, q, s, i, place, neighbour).start())
                        pl.when(odd == 1)(lambda: scatter(hf, q, s, i))
                    else:
                        scatter(hf, q, s, i)

            if s < 3:
                act()
            else:
                pl.when(odd == 0)(act)

        loop(0, 4, step)

    def scatter(hf, q, s, i):
        to = (y + 1 - 2 * (i % 2) + N) % N
        for j in range(4):
            remote(
                ring_send.at[0, q, s, 16 * j : 16 * j + 16], sum_in.at[hf, i % 2, c], S_R, last_recv.at[hf],
                dev(to, z, i // 2 * 4 + j),
            ).start()

    def scatter_own(hf):
        own_out[hf] = pre_own[hf, y].astype(BF16)

        def start(k):
            to = (c + k) % N
            remote(own_out.at[hf, to], sum_in.at[hf, 2, c], S_HC, own_recv.at[hf], dev(y, z, to)).start()

        loop(1, N, start)
        sum_in[hf, 2, c] = own_out[hf, c]

    def ring_last(hf, p, ring):
        at, place, _, own = ring
        total = own(hf, place, p)
        for i in (2 * p, 2 * p + 1):
            q, s = hf * 4 + i, 3 - (p + i % 2) % 2
            take(ring_recv.at[at, q, s], rs_recv.at[at, q, s])
            total = total + ring_recv[at, q, s].astype(F32)
        return total.reshape(4, 16, 384)

    def along_y(to):
        return dev(to, z, c)

    def along_z(to):
        return dev(y, to, c)

    FIRST, LATER = (4, 3, 5), (2, 6, 1, 7, 0)

    def pre_product(hf, offsets):
        for off in offsets:
            at = (y + off) % N
            sums = jnp.dot(rows_of(x_buf[hf, at]), rows_of(w1[...]), preferred_element_type=F32)
            pre_own[hf, at] = sums.reshape(N, 16, 384)

    def out_product(hf, offsets):
        for off in offsets:
            at = (y + off) % N
            sums = jnp.dot(rows_of(h_buf[hf, :, at]), w2[0], preferred_element_type=F32)
            out_own[0, hf, at] = sums.reshape(N, 16, 384)
            at = (z + off) % N
            sums = jnp.dot(rows_of(h_buf[hf, at]), w2[1], preferred_element_type=F32)
            out_own[1, hf, at] = sums.reshape(N, 16, 384)

    def pre_part(hf, to, p):
        return rows_of(pre_own[hf, to, pl.ds(4 * p, 4)])

    def out_part_a(hf, to, p):
        return rows_of(out_own[0, hf, to, pl.ds(4 * p, 4)])

    def out_part_b(hf, to, p):
        return rows_of(out_own[1, hf, to, pl.ds(4 * p, 4)])

    ring_pre = (0, y, along_y, pre_part)
    ring_out = ((1, y, along_y, out_part_a), (2, z, along_z, out_part_b))

    def pass_on(hf, of):
        remote(hid_in.at[hf, of], h_buf.at[hf, c, y], S_HY, hy_recv.at[hf, y], dev(of, z, c)).start()

    def hidden(hf):
        take(sum_in.at[hf, 0:2], last_recv.at[hf])
        take(sum_in.at[hf, 2, 0:7], own_recv.at[hf])
        total = sum_in[hf, 0].astype(F32) + sum_in[hf, 1].astype(F32) + sum_in[hf, 2].astype(F32)
        hid_in[hf] = gelu(total).astype(BF16)
        loop(1, N, lambda k: pass_on(hf, (y + far_first(k)) % N))
        h_buf[hf, c, y] = hid_in[hf, y]

    others = ((z, along_z), (y, along_y))

    def rest_of_sum(hf):
        def send(j, to):
            place, neighbour = others[j]

            @pl.when(to != place)
            def _():
                remote(part.at[j, hf, to], part_in.at[j, hf, place], S_P, p_recv.at[j, hf], neighbour(to)).start()

        for p in range(2):
            for j in range(2):
                total = ring_last(hf, p, ring_out[j])
                own_part[j, hf, 4 * p : 4 * p + 4] = total
                part[j, hf, 4 * p : 4 * p + 4] = total.astype(BF16)
                for to in range(4 * p, 4 * p + 4):
                    send(j, to)

    def finish(hf):
        for j, (place, _) in enumerate(others):
            take(part_in.at[j, hf, 0:7], p_recv.at[j, hf])
            total = own_part[j, hf, place]
            for k in range(1, N):
                total = total + part_in[j, hf, (place + k) % N].astype(F32)
            slab[16 * hf : 16 * hf + 16, 384 * j : 384 * (j + 1)] = total
        for p in range(4 * hf, 4 * hf + 4):
            fin_out[p] = slab[4 * p : 4 * p + 4].astype(BF16)

            @pl.when(jnp.logical_and(y == c, p == y))
            def _():
                fin_in[c] = fin_out[p]

            @pl.when(jnp.logical_or(y != c, p != y))
            def _():
                remote(fin_out.at[p], fin_in.at[c], S_F, f_recv, dev(p, z, y)).start()

    gx, gh = Gather(x_buf, S_X, x_recv), Gather(h_buf, S_H, h_recv)
    x_own(0)
    x_own(1)
    gx.near(0)
    gx.far(0)
    gx.rest(0)
    own_w1.wait()
    take(w1.at[0:7], w_recv)
    pre_product(0, FIRST)
    rings(0, 0, [ring_pre])
    pre_product(0, LATER)
    gx.near(1)
    gx.far(1)
    rings(0, 1, [ring_pre])
    scatter_own(0)
    gx.rest(1)
    pre_product(1, FIRST)
    rings(1, 0, [ring_pre])
    pre_product(1, LATER)
    rings(0, 2, [ring_pre])
    rings(1, 1, [ring_pre])
    scatter_own(1)
    rings(0, 3, [ring_pre])
    rings(1, 2, [ring_pre])
    hidden(0)
    rings(1, 3, [ring_pre])
    for copy in own_w2:
        copy.wait()
    h_own(0)
    hidden(1)
    def pass_half_0():
        gh.near(0)
        gh.far(0)

    h_own(1, pass_half_0)
    gh.rest(0)
    out_product(0, FIRST)
    rings(0, 0, ring_out)
    out_product(0, LATER)
    gh.near(1)
    gh.far(1)
    rings(0, 1, ring_out)
    gh.rest(1)
    out_product(1, FIRST)
    rings(1, 0, ring_out)
    out_product(1, LATER)
    rings(0, 2, ring_out)
    rings(1, 1, ring_out)
    rings(0, 3, ring_out)
    rings(1, 2, ring_out)
    rest_of_sum(0)
    rings(1, 3, ring_out)
    rest_of_sum(1)
    finish(0)
    finish(1)

    drain(norm_out.at[0:7], S_Y)
    drain(w1.at[0:7], S_W)
    drain(x_buf.at[:, 0, 0:7], S_Z)
    for hf in range(2):
        drain(x_buf.at[hf, 0:7], S_X + hf)
        drain(h_buf.at[hf, 0:7], S_H + hf)
    for at in range(3):
        drain(ring_send.at[at, 0:7], S_R + at)
    drain(own_out.at[:, 0:7], S_HC)
    drain(hid_in.at[:, 0:7], S_HY)
    drain(part.at[:, :, 0:7], S_P)

    @pl.when(y == c)
    def _():
        drain(fin_out.at[0:7], S_F)
        take(fin_in.at[0:7], f_recv)

    @pl.when(y != c)
    def _():
        drain(fin_out, S_F)
        take(fin_in, f_recv)

    for j in range(N):
        cols = slice(768 * j, 768 * (j + 1))
        out_ref[:, cols] = (tok_ref[:, cols].astype(F32) + fin_in[j].astype(F32)).astype(BF16)


def body(tokens, norm_gain, in_weight, out_weight):
    dma = pltpu.SemaphoreType.DMA
    return pl.pallas_call(
        kernel,
        out_shape=jax.ShapeDtypeStruct(tokens.shape, BF16),
        in_specs=[pl.BlockSpec(memory_space=pltpu.HBM)] * 4,
        out_specs=pl.BlockSpec(memory_space=pltpu.VMEM),
        scratch_shapes=[
            pltpu.VMEM((4, 6144), BF16),
            pltpu.VMEM((1, 6144), F32),
            pltpu.VMEM((N, 96, 384), BF16),
            pltpu.VMEM((2, 384, 384), BF16),
            pltpu.VMEM((N, 4, 768), BF16),
            pltpu.VMEM((N, 4, 768), BF16),
            pltpu.VMEM((32, 768), F32),
            pltpu.VMEM((2, N, N, 16, 768), BF16),
            pltpu.VMEM((2, N, N, 16, 384), F32),
            pltpu.VMEM((2, N, 16, 384), BF16),
            pltpu.VMEM((2, 3, N, 16, 384), BF16),
            pltpu.VMEM((2, N, 16, 384), BF16),
            pltpu.VMEM((2, N, N, 16, 384), BF16),
            pltpu.VMEM((2, 2, N, N, 16, 384), F32),
            pltpu.VMEM((3, 8, 4, 64, 384), BF16),
            pltpu.VMEM((3, 8, 4, 64, 384), BF16),
            pltpu.VMEM((2, 2, N, 16, 384), BF16),
            pltpu.VMEM((2, 2, N, 16, 384), BF16),
            pltpu.VMEM((2, 2, N, 16, 384), F32),
            pltpu.VMEM((N, 4, 768), BF16),
            pltpu.VMEM((N, 4, 768), BF16),
            dma((5,)), dma((SENDS,)), dma, dma, dma((2, N)), dma((2, 4)), dma((2, 4)), dma((2,)), dma((2,)), dma((2, N)),
            dma((3, 8, 4)), dma((2, 2)), dma,
        ],
        compiler_params=pltpu.CompilerParams(
            collective_id=0, has_side_effects=True, vmem_limit_bytes=62 * 1024 * 1024
        ),
        cost_estimate=pl.CostEstimate(flops=2_500_000_000, bytes_accessed=1_300_000, transcendentals=100_000),
    )(tokens, norm_gain.reshape(1, -1), in_weight, out_weight)


def solution(mesh):
    return jax.shard_map(
        body,
        mesh=mesh,
        in_specs=(P(("row", "col"), None), P(), P("row", "col"), P("row", "col")),
        out_specs=P(("row", "col"), None),
        check_vma=False,
    )
```
